128 devices in a mesh: prow: 8 (over z, core), pcol: 16 (over x, y).
Axes of the slice: x: 4, y: 4, z: 4, core: 2. Of those that a mesh axis runs over, the one named last changes fastest.
Arguments:
- child_inverse: float32 [8, 16, 8, 256, 256], P('prow', 'pcol'), as said below
- child_rhs: float32 [8, 16, 8, 256, 256], P('prow', 'pcol'), may hold values from -6 to 6
- panels: float32 [8, 16, 8, 128, 256], P('prow', 'pcol'), may hold values from -0.125 to 0.125
- panel_parent: int32 [8, 16, 8, 1], P('prow', 'pcol'), may hold values from 0 to 15; in each aligned block of 8 rows (0 to 7, 8 to 15, ..., all dimensions but the last counted through in order) no two rows name the same one
- panel_rows: int32 [8, 16, 8, 128], P('prow', 'pcol'), may hold values from 0 to 255, as said below
- parent_inverse: float32 [8, 16, 256, 256], P('prow', 'pcol'), as said below
- parent_rhs: float32 [8, 16, 256, 256], P('prow', 'pcol'), may hold values from -6 to 6
Outputs:
- child_solution: float32 [8, 16, 8, 256, 256], P('prow', 'pcol')
- parent_solution: float32 [8, 16, 256, 256], P('prow', 'pcol')
The draws below stay inside these ranges and needn't reach their ends.
Inputs may be any that keep to these rules, and one draw needn't show every extreme that they name: `panel_parent`: in the 8 slots of one device no parent is named more than 1 times. `panel_rows`: each slot lists 128 different columns of its parent in ascending order. `child_inverse`: lower triangular, with diagonal entries between 0.4 and 2.1. `parent_inverse`: lower triangular, with diagonal entries between 0.4 and 2.1.
All inputs are finite; a program needn't handle non-finite values.
Results may differ from the reference program's by a relative error of at most 0.00005.
Values sent between devices are 32-bit elements; how exact they have to be, the bound alone decides.
A program may use at most 64 MiB of HBM per device.

```python
import math
import jax
import jax.numpy as jnp
import numpy as np
from jax import lax

W = 256
R = 128
NRHS = 256
CH_DEV = 8
PROWS = 8
PCOLS = 16
MOST = 1


def triangle(below_diag, diagonal):
    order_size = below_diag.shape[-1]
    lower_part = jnp.tril(below_diag, -1)
    return lower_part + diagonal[..., None] * jnp.eye(order_size, dtype=jnp.float32)


def draw_child_inverse(key, part):
    key = jax.random.fold_in(key, 11)
    leading = (PROWS, PCOLS, CH_DEV)
    below_key, diagonal_key = jax.random.split(key)
    below_diag = jax.random.normal(below_key, leading + (W, W), jnp.float32) * (0.6 / math.sqrt(W))
    diagonal = jnp.exp(jax.random.uniform(diagonal_key, leading + (W,), jnp.float32, -0.5, 0.5))
    return triangle(below_diag, diagonal)


def draw_parent_inverse(key, part):
    key = jax.random.fold_in(key, 23)
    leading = (PROWS, PCOLS)
    below_key, diagonal_key = jax.random.split(key)
    below_diag = jax.random.normal(below_key, leading + (W, W), jnp.float32) * (0.6 / math.sqrt(W))
    diagonal = jnp.exp(jax.random.uniform(diagonal_key, leading + (W,), jnp.float32, -0.5, 0.5))
    return triangle(below_diag, diagonal)


def chosen_rows(row_key):
    return jnp.sort(jax.random.permutation(row_key, W)[:R]).astype(jnp.int32)


def draw_panel_rows(key, part):
    key = jax.random.fold_in(key, 37)
    row_keys = jax.random.split(key, PROWS * PCOLS * CH_DEV)
    listed = jax.vmap(chosen_rows)(row_keys)
    return listed.reshape(PROWS, PCOLS, CH_DEV, R).astype(jnp.int32)


def levels(own_key, dims, pieces, smallest, high):
    def one(position, blocks):
        steps = jax.random.uniform(jax.random.fold_in(jax.random.fold_in(own_key, 6), position), (blocks,), jnp.float32, smallest / len(pieces), high / len(pieces))
        return jnp.repeat(jnp.exp(steps), dims[position] // blocks).reshape((-1,) + (1,) * (len(dims) - position - 1))

    level = one(*pieces[0])
    for cut in pieces[1:]:
        level = level * one(*cut)
    return level


def routed_block(own_key, own, number, rows, number_of, top, limit, lean):
    order = jax.random.permutation(own_key, number_of)
    heavy_load, usual = load_shares(number_of, rows * top, limit, lean, True), load_shares(number_of, rows * top, limit, lean, False)
    places = jnp.arange(number_of)

    def named(tallies, rotation):
        used = int((tallies > 0).sum())
        fixed = max(1, used // 4)
        passed = fixed + (places - fixed + rotation * (used - fixed)) % max(1, number_of - fixed)
        return jnp.zeros((number_of,), jnp.int32).at[order[jnp.where(places < fixed, places, passed)]].set(jnp.asarray(tallies, jnp.int32))

    tallies = jnp.where(number % 4 == 0, named(heavy_load, number // 4), named(usual, number - number // 4 - 1))
    mixed = jax.random.permutation(jax.random.fold_in(own, 3), number_of)
    giver, receiver = mixed[0:number_of // 2 * 2:2], mixed[1:number_of // 2 * 2:2]
    slack = jnp.minimum(tallies[giver] - 1, limit - tallies[receiver]) // 2
    slack = jnp.where((giver == order[0]) | (receiver == order[0]) | (tallies[receiver] == 0), 0, jnp.maximum(slack, 0))
    passed = jax.random.randint(jax.random.fold_in(own, 4), (number_of // 2,), 0, 1 << 20) % (slack + 1)
    tallies = tallies.at[giver].add(-passed).at[receiver].add(passed)
    items = jnp.searchsorted(jnp.cumsum(tallies), jnp.arange(rows * top), side="right").astype(jnp.int32)
    listing = items.reshape(top, rows).T
    listing = listing[jax.random.permutation(jax.random.fold_in(own, 1), rows)]
    rotation = jax.random.randint(jax.random.fold_in(own, 2), (rows, 1), 0, top)
    return jnp.take_along_axis(listing, (jnp.arange(top)[None, :] + rotation) % top, axis=1)


def load_shares(number_of, total, limit, skew, full):
    weights = [(1 << 20) // math.isqrt(rank ** skew) + 1 for rank in range(1, number_of + 1)]
    largest = limit if full else min(limit, max(-(-total // number_of), total * weights[0] // sum(weights)))
    least = 1 if total - largest >= number_of - 1 else 0
    holding, surplus = [largest] + [least] * (number_of - 1), total - largest - least * (number_of - 1)
    while surplus > 0:
        movable = [i for i in range(1, number_of) if holding[i] < largest] or [i for i in range(1, number_of) if holding[i] < limit]
        pool, budget = sum([weights[i] for i in movable]), surplus
        for i in movable:
            addition = min(limit - holding[i], max(1, budget * weights[i] // pool), surplus)
            holding[i] = holding[i] + addition
            surplus = surplus - addition
    return np.array(holding)


def bell_draw(key, dims, spread, most, cuts=(), kind=jnp.bfloat16):
    gain = levels(key, dims, cuts, -0.22, 0.18) if cuts else 1.0
    result = jax.random.normal(key, dims, jnp.float32) * spread * gain
    return jnp.minimum(jnp.maximum(result, -most), most).astype(kind)


def setup_inputs(seed: int = 0) -> dict:
    splits = jax.random.split(jax.random.key(seed), 8)
    child_inverse = draw_child_inverse(jax.random.fold_in(splits[7], 71), 0)
    child_rhs = bell_draw(splits[1], (PROWS, PCOLS, CH_DEV, W, NRHS), 1.0, 6.0, ((0, 8), (1, 16)), jnp.float32)
    panels = bell_draw(splits[2], (PROWS, PCOLS, CH_DEV, R, W), (10 * W) ** -0.5, 0.125, ((0, 8), (1, 16)), jnp.float32)
    panel_parent_keys = jax.random.split(jax.random.fold_in(splits[3], 1), PROWS * PCOLS * CH_DEV // CH_DEV)
    panel_parent_turns = jax.random.permutation(jax.random.fold_in(splits[3], 3), PROWS * PCOLS * CH_DEV // CH_DEV)
    panel_parent = jax.vmap(lambda own, number: routed_block(jax.random.fold_in(splits[3], 2), own, number, CH_DEV, PCOLS, 1, MOST, 2))(panel_parent_keys, panel_parent_turns).reshape((PROWS, PCOLS, CH_DEV, 1))
    panel_rows = draw_panel_rows(jax.random.fold_in(splits[7], 71), 0)
    parent_inverse = draw_parent_inverse(jax.random.fold_in(splits[7], 71), 0)
    parent_rhs = bell_draw(splits[6], (PROWS, PCOLS, W, NRHS), 1.0, 6.0, ((0, 8), (1, 16)), jnp.float32)
    return dict(child_inverse=child_inverse, child_rhs=child_rhs, panels=panels, panel_parent=panel_parent, panel_rows=panel_rows, parent_inverse=parent_inverse, parent_rhs=parent_rhs)


highest = lax.Precision.HIGHEST


def regroup(values):
    group_size = CH_DEV // PROWS
    trailing = values.shape[3:]
    blocked = values.reshape((PROWS, PCOLS, PROWS, group_size) + trailing)
    permuted = (2, 1, 0, 3) + tuple(range(4, 4 + len(trailing)))
    return jnp.transpose(blocked, permuted).reshape((PROWS, PCOLS, CH_DEV) + trailing)


def add_rows(indices, updates):
    initial = jnp.zeros((PCOLS * W, NRHS), jnp.float32)
    return initial.at[indices].add(updates)


def take_rows(source, indices):
    return source[indices]


def reference(child_inverse, child_rhs, panels, panel_parent, panel_rows, parent_inverse, parent_rhs):
    y_child = jnp.einsum("rqkab,rqkbn->rqkan", child_inverse, child_rhs, precision=highest)
    y_panel = regroup(y_child)
    update = jnp.einsum("iqsra,iqsan->iqsrn", panels, y_panel, precision=highest)
    target = panel_parent.astype(jnp.int32) * W + panel_rows.astype(jnp.int32)
    target = target.reshape(PROWS, PCOLS * CH_DEV * R)
    parent_sum = jax.vmap(add_rows)(target, update.reshape(PROWS, PCOLS * CH_DEV * R, NRHS))
    parent_sum = parent_sum.reshape(PROWS, PCOLS, W, NRHS)
    y_parent = jnp.einsum("iqab,iqbn->iqan", parent_inverse, parent_rhs - parent_sum, precision=highest)
    parent_solution = jnp.einsum("iqba,iqbn->iqan", parent_inverse, y_parent, precision=highest)
    gathered = jax.vmap(take_rows)(parent_solution.reshape(PROWS, PCOLS * W, NRHS), target)
    gathered = gathered.reshape(PROWS, PCOLS, CH_DEV, R, NRHS)
    correction = jnp.einsum("iqsra,iqsrn->iqsan", panels, gathered, precision=highest)
    child_solution = jnp.einsum("rqkba,rqkbn->rqkan", child_inverse, y_child - regroup(correction), precision=highest)
    return child_solution, parent_solution
```

```python
import jax
import jax.numpy as jnp
from jax import lax
from jax.experimental import pallas as pl
from jax.experimental.pallas import tpu as pltpu
from jax.sharding import PartitionSpec as P

MESH = pl.DeviceIdType.MESH
F32 = jnp.float32
BF16 = jnp.bfloat16
W = 256
R = 128
CH = 8
C = 2
CW = 128
DMA = pltpu.SemaphoreType.DMA


def split(value):
    high = value.astype(BF16)
    low = (value - high.astype(F32)).astype(BF16)
    return high, low


def dot(a, b, dims=((1,), (0,))):
    return lax.dot_general(a, b, (dims, ((), ())), preferred_element_type=F32)


def product(a, b, dims=((1,), (0,))):
    a_high, a_low = split(a)
    b_high, b_low = split(b)
    return dot(a_high, b_high, dims) + (dot(a_high, b_low, dims) + dot(a_low, b_high, dims))


def chosen(one_hot, b):
    b_high, b_low = split(b)
    return dot(one_hot, b_high) + dot(one_hot, b_low)


def kernel(
    parent_ids, inverse_hbm, rhs_hbm, panels_hbm, rows_ref, pinv_ref, prhs_ref,
    child_out, parent_out,
    inverse, rhs, panels, y_send, y_in, update, rows_send, rows_in, one_hot, one_hot_t,
    first_send, first_in, dense, second_in, k_high, k_low, z_parent, x_block, pick_send, pick_in_0, pick_in_1,
    v_send, v_in, panel_in, gain_high, gain_low, z_child, out_buf,
    load_sem, out_sem, y_s, y_r, p_s, p_r, i_s, i_r, s1_s, s1_r, s2_s, s2_r, t1_s, t1_r, t2_s, t2_r, v_s, v_r,
):
    r = lax.axis_index("prow")
    q = lax.axis_index("pcol")
    core = r % 2
    x, y = q // 4, q % 4
    cls = (x + y + core) % 2
    own_pos = jnp.where(cls == 0, y, x)
    other_pos = jnp.where(cls == 0, x, y)
    t_self = own_pos // 2
    first_pos = (x, y)
    pick_in = (pick_in_0, pick_in_1)

    def first_dev(f, a):
        return (r, a * 4 + y) if f == 0 else (r, x * 4 + a)

    def own_dev(a):
        return (r, jnp.where(cls == 0, x * 4 + a, a * 4 + y))

    def other_dev(a):
        return (r, jnp.where(cls == 0, a * 4 + y, x * 4 + a))

    def remote(src, dst, send, recv, dev):
        return pltpu.make_async_remote_copy(
            src_ref=src, dst_ref=dst, send_sem=send, recv_sem=recv, device_id=dev, device_id_type=MESH
        )

    barrier = pltpu.get_barrier_semaphore()

    def greet(j, carry):
        pl.semaphore_signal(barrier, inc=1, device_id=((r + j) % 8, q), device_id_type=MESH)
        return carry

    lax.fori_loop(1, 8, greet, 0)
    for f in range(2):
        for d in range(1, 4):
            pl.semaphore_signal(barrier, inc=1, device_id=first_dev(f, (first_pos[f] + d) % 4), device_id_type=MESH)

    def load(k):
        return (
            pltpu.make_async_copy(inverse_hbm.at[k], inverse.at[k], load_sem.at[0, k]),
            pltpu.make_async_copy(rhs_hbm.at[k], rhs.at[k], load_sem.at[1, k]),
        )

    def start_load(j, carry):
        for copy in load((r + 1 + j) % 8):
            copy.start()
        return carry

    lax.fori_loop(0, 8, start_load, 0)
    panel_load = pltpu.make_async_copy(panels_hbm, panels, load_sem.at[2, 0])
    panel_load.start()

    def y_copy(c, k):
        return remote(y_send.at[c, k], y_in.at[c, r], y_s.at[c, k], y_r.at[c, r], (k, q))

    def y_wait(c, s):
        return remote(y_send.at[c, s], y_in.at[c, s], y_s.at[c, s], y_r.at[c, s], (s, q))

    def forward(k):
        for copy in load(k):
            copy.wait()
        value = product(inverse[k], rhs[k])
        for c in range(C):
            y_send[c, k] = value[:, c * CW:(c + 1) * CW]

    forward((r + 1) % 8)
    pl.semaphore_wait(barrier, 13)
    y_copy(0, (r + 1) % 8).start()

    def forward_step(j, carry):
        k = (r + j) % 8
        forward(k)
        y_copy(0, k).start()
        return carry

    lax.fori_loop(2, 8, forward_step, 0)
    forward(r)
    for c in range(C):
        y_in[c, r] = y_send[c, r]

    def parent_of(f, a, t):
        if f == 0:
            return a * 4 + (a + core) % 2 + 2 * t
        return ((a + core + 1) % 2 + 2 * t) * 4 + a

    def rows_copy(f, a):
        return remote(rows_send.at[f, a], rows_in.at[f, first_pos[f]], i_s.at[f, a], i_r.at[f, first_pos[f]], first_dev(f, a))

    def rows_wait(f, a):
        return remote(rows_send.at[f, a], rows_in.at[f, a], i_s.at[f, a], i_r.at[f, a], first_dev(f, a))

    for f in range(2):
        for a in range(4):
            for t in range(2):
                p = parent_of(f, a, t)
                listed = jnp.full((1, R), -1, jnp.int32)
                for s in range(CH):
                    listed = jnp.where(parent_ids[s] == p, rows_ref[s:s + 1, :], listed)
                rows_send[f, a, t:t + 1, :] = listed
            rows_send[f, a, 2:8, :] = jnp.zeros((6, R), jnp.int32)
        rows_in[f, first_pos[f]] = rows_send[f, first_pos[f]]
        for d in range(1, 4):
            rows_copy(f, (first_pos[f] + d) % 4).start()

    def y_next(j, carry):
        k = (r + j) % 8
        y_copy(0, k).wait_send()
        y_copy(1, k).start()
        return carry

    lax.fori_loop(1, 8, y_next, 0)

    gram = product(pinv_ref[...], pinv_ref[...], ((0,), (0,)))
    high, low = split(gram)
    k_high[...] = high
    k_low[...] = low
    value = product(gram, prhs_ref[...])
    for c in range(C):
        z_parent[c] = value[:, c * CW:(c + 1) * CW]

    for f in range(2):
        for d in range(1, 4):
            rows_wait(f, (first_pos[f] + d) % 4).wait_recv()
        for a in range(4):
            for t in range(2):
                listed = rows_in[f, a, t:t + 1, :]
                places = lax.broadcasted_iota(jnp.int32, (W, R), 0)
                matrix = jnp.where(places == listed, 1.0, 0.0).astype(F32)
                one_hot[f, t, :, a * R:(a + 1) * R] = matrix.astype(BF16)
                one_hot_t[f, t, a * R:(a + 1) * R, :] = matrix.T.astype(BF16)
    panel_load.wait()

    def first_copy(c, f, a):
        return remote(first_send.at[c, f, a], first_in.at[c, f, first_pos[f]], s1_s.at[c, f, a], s1_r.at[c, f, first_pos[f]], first_dev(f, a))

    def first_wait(c, f, a):
        return remote(first_send.at[c, f, a], first_in.at[c, f, a], s1_s.at[c, f, a], s1_r.at[c, f, a], first_dev(f, a))

    def step_update(c):
        def one(j, carry):
            s = (r + j) % 8
            y_wait(c, s).wait_recv()
            update[c, s] = product(panels[s], y_in[c, s])
            return carry

        update[c, r] = product(panels[r], y_in[c, r])
        lax.fori_loop(1, 8, one, 0)
        for f in range(2):
            for a in range(4):
                for t in range(2):
                    p = parent_of(f, a, t)
                    slot = jnp.int32(0)
                    for s in range(1, CH):
                        slot = jnp.where(parent_ids[s] == p, s, slot)
                    first_send[c, f, a, t] = update[c, slot]
            first_in[c, f, first_pos[f]] = first_send[c, f, first_pos[f]]
            for d in (2, 1, 3):
                first_copy(c, f, (first_pos[f] + d) % 4).start()

    def second_own(c):
        a = (own_pos + 2) % 4
        return remote(dense.at[c, cls, 1 - t_self], second_in.at[c, own_pos], s2_s.at[c, 2], s2_r.at[c, own_pos], own_dev(a))

    def second_other(c, t):
        a = (other_pos + 1) % 2 + 2 * t
        return remote(dense.at[c, 1 - cls, t], second_in.at[c, other_pos], s2_s.at[c, t], s2_r.at[c, other_pos], other_dev(a))

    def second_wait(c, a):
        return remote(dense.at[c, 0, 0], second_in.at[c, a], s2_s.at[c, 0], s2_r.at[c, a], own_dev(a))

    def step_dense(c):
        for f in range(2):
            for d in (1, 3, 2):
                first_wait(c, f, (first_pos[f] + d) % 4).wait_recv()
            for t in range(2):
                blocks = first_in[c, f, :, t].reshape(4 * R, CW)
                dense[c, f, t] = chosen(one_hot[f, t], blocks)
        second_own(c).start()
        for t in range(2):
            second_other(c, t).start()

    def x_copy(c, d):
        return remote(x_block.at[c, cls, t_self], x_block.at[c, cls, t_self], t1_s.at[c, d], t1_r.at[c, cls, t_self], own_dev((own_pos + d) % 4))

    def x_wait_own(c):
        return remote(x_block.at[c, cls, 1 - t_self], x_block.at[c, cls, 1 - t_self], t1_s.at[c, 1], t1_r.at[c, cls, 1 - t_self], own_dev((own_pos + 2) % 4))

    def x_wait_other(c, t):
        a = (other_pos + 1) % 2 + 2 * t
        return remote(x_block.at[c, 1 - cls, t], x_block.at[c, 1 - cls, t], t1_s.at[c, 1], t1_r.at[c, 1 - cls, t], other_dev(a))

    def step_parent(c):
        total = dense[c, cls, t_self]
        for d in (1, 3, 2):
            a = (own_pos + d) % 4
            second_wait(c, a).wait_recv()
            total = total + second_in[c, a]
        high, low = split(total)
        k_h = k_high[...]
        solution_block = z_parent[c] - (dot(k_h, high) + (dot(k_h, low) + dot(k_low[...], high)))
        x_block[c, cls, t_self] = solution_block
        for d in (2, 1, 3):
            x_copy(c, d).start()
        parent_out[:, c * CW:(c + 1) * CW] = solution_block

    def pick_copy(c, f, a):
        return remote(pick_send.at[c, f, a], pick_in[c].at[f, first_pos[f]], t2_s.at[c, f, a], t2_r.at[c, f, first_pos[f]], first_dev(f, a))

    def pick_wait(c, f, a):
        return remote(pick_send.at[c, f, a], pick_in[c].at[f, a], t2_s.at[c, f, a], t2_r.at[c, f, a], first_dev(f, a))

    def step_pick(c):
        for t in range(2):
            x_wait_other(c, t).wait_recv()
        x_wait_own(c).wait_recv()
        for f in range(2):
            for t in range(2):
                picked = chosen(one_hot_t[f, t], x_block[c, f, t])
                pick_send[c, f, :, t] = picked.reshape(4, R, CW)
            pick_in[c][f, first_pos[f]] = pick_send[c, f, first_pos[f]]
            for d in (2, 1, 3):
                pick_copy(c, f, (first_pos[f] + d) % 4).start()

    def v_copy(c, s):
        return remote(v_send.at[c, s], v_in.at[c, r], v_s.at[c, s], v_r.at[c, r], (s, q))

    def v_wait(c, s):
        return remote(v_send.at[c, s], v_in.at[c, s], v_s.at[c, s], v_r.at[c, s], (s, q))

    def step_return(c):
        for f in range(2):
            for d in (1, 3, 2):
                pick_wait(c, f, (first_pos[f] + d) % 4).wait_recv()

        def one(j, carry):
            s = (r + j) % 8
            p = parent_ids[s]
            x_p, y_p = p // 4, p % 4
            f = (x_p + y_p + core) % 2
            a = jnp.where(f == 0, x_p, y_p)
            t = jnp.where(f == 0, y_p, x_p) // 2
            v_send[c, s] = pick_in[c][f, a, t]
            return carry

        lax.fori_loop(0, 8, one, 0)

        def begin(j, carry):
            v_copy(c, (r + j) % 8).start()
            return carry

        lax.fori_loop(1, 8, begin, 0)
        v_in[c, r] = v_send[c, r]

    def panel_copy(k):
        return remote(panels.at[k], panel_in.at[r], p_s.at[k], p_r.at[r], (k, q))

    def panel_wait(s):
        return remote(panels.at[s], panel_in.at[s], p_s.at[s], p_r.at[s], (s, q))

    def send_panels():
        def one(j, carry):
            k = (r + j) % 8
            y_copy(1, k).wait_send()
            panel_copy(k).start()
            return carry

        lax.fori_loop(1, 8, one, 0)
        panel_in[r] = panels[r]

    def gains():
        def one(j, carry):
            s = (r + j) % 8

            @pl.when(j > 0)
            def _():
                panel_wait(s).wait_recv()

            high, low = split(product(panel_in[s], inverse[s]).T)
            gain_high[s] = high
            gain_low[s] = low
            return carry

        lax.fori_loop(0, 8, one, 0)

    def solved():
        def one(k, carry):
            i_high, i_low = split(inverse[k].T)
            for c in range(C):
                y_high, y_low = split(y_send[c, k])
                z_child[c, k] = dot(i_high, y_high) + (dot(i_high, y_low) + dot(i_low, y_high))
            return carry

        lax.fori_loop(0, 8, one, 0)

    def out_copy(c, k):
        return pltpu.make_async_copy(out_buf.at[k, :, pl.ds(c * CW, CW)], child_out.at[k, :, pl.ds(c * CW, CW)], out_sem.at[c, k])

    def step_final(c):
        def one(j, carry):
            s = (r + j) % 8

            @pl.when(j > 0)
            def _():
                v_wait(c, s).wait_recv()

            high, low = split(v_in[c, s])
            g_high = gain_high[s]
            value = z_child[c, s] - (dot(g_high, high) + (dot(g_high, low) + dot(gain_low[s], high)))
            out_buf[s, :, c * CW:(c + 1) * CW] = value
            out_copy(c, s).start()
            return carry

        lax.fori_loop(0, 8, one, 0)

    step_update(0)
    solved()
    step_dense(0)
    step_parent(0)
    send_panels()
    step_update(1)
    step_pick(0)
    step_dense(1)
    step_parent(1)
    step_return(0)
    step_pick(1)
    gains()
    step_return(1)
    step_final(0)
    step_final(1)

    def z_done(j, carry):
        k = (r + j) % 8
        panel_copy(k).wait_send()
        for c in range(C):
            v_copy(c, k).wait_send()
        return carry

    lax.fori_loop(1, 8, z_done, 0)
    for f in range(2):
        for d in range(1, 4):
            a = (first_pos[f] + d) % 4
            rows_copy(f, a).wait_send()
            for c in range(C):
                first_copy(c, f, a).wait_send()
                pick_copy(c, f, a).wait_send()
    for c in range(C):
        second_own(c).wait_send()
        for t in range(2):
            second_other(c, t).wait_send()
        for d in range(1, 4):
            x_copy(c, d).wait_send()

    def out_done(k, carry):
        for c in range(C):
            out_copy(c, k).wait()
        return carry

    lax.fori_loop(0, 8, out_done, 0)


def body(child_inverse, child_rhs, panels, panel_parent, panel_rows, parent_inverse, parent_rhs):
    vmem = pl.BlockSpec(memory_space=pltpu.VMEM)
    anywhere = pl.BlockSpec(memory_space=pl.ANY)
    child, parent = pl.pallas_call(
        kernel,
        out_shape=(jax.ShapeDtypeStruct((CH, W, W), F32), jax.ShapeDtypeStruct((W, W), F32)),
        in_specs=[pl.BlockSpec(memory_space=pltpu.SMEM), anywhere, anywhere, anywhere, vmem, vmem, vmem],
        out_specs=(anywhere, vmem),
        scratch_shapes=[
            pltpu.VMEM((CH, W, W), F32),
            pltpu.VMEM((CH, W, W), F32),
            pltpu.VMEM((CH, R, W), F32),
            pltpu.VMEM((C, CH, W, CW), F32),
            pltpu.VMEM((C, CH, W, CW), F32),
            pltpu.VMEM((C, CH, R, CW), F32),
            pltpu.VMEM((2, 4, 8, R), jnp.int32),
            pltpu.VMEM((2, 4, 8, R), jnp.int32),
            pltpu.VMEM((2, 2, W, 4 * R), BF16),
            pltpu.VMEM((2, 2, 4 * R, W), BF16),
            pltpu.VMEM((C, 2, 4, 2, R, CW), F32),
            pltpu.VMEM((C, 2, 4, 2, R, CW), F32),
            pltpu.VMEM((C, 2, 2, W, CW), F32),
            pltpu.VMEM((C, 4, W, CW), F32),
            pltpu.VMEM((W, W), BF16),
            pltpu.VMEM((W, W), BF16),
            pltpu.VMEM((C, W, CW), F32),
            pltpu.VMEM((C, 2, 2, W, CW), F32),
            pltpu.VMEM((C, 2, 4, 2, R, CW), F32),
            pltpu.VMEM((2, 4, 2, R, CW), F32),
            pltpu.VMEM((2, 4, 2, R, CW), F32),
            pltpu.VMEM((C, CH, R, CW), F32),
            pltpu.VMEM((C, CH, R, CW), F32),
            pltpu.VMEM((CH, R, W), F32),
            pltpu.VMEM((CH, W, R), BF16),
            pltpu.VMEM((CH, W, R), BF16),
            pltpu.VMEM((C, CH, W, CW), F32),
            pltpu.VMEM((CH, W, W), F32),
            DMA((3, CH)),
            DMA((C, CH)),
            DMA((C, CH)), DMA((C, CH)),
            DMA((CH,)), DMA((CH,)),
            DMA((2, 4)), DMA((2, 4)),
            DMA((C, 2, 4)), DMA((C, 2, 4)),
            DMA((C, 3)), DMA((C, 4)),
            DMA((C, 4)), DMA((C, 2, 2)),
            DMA((C, 2, 4)), DMA((C, 2, 4)),
            DMA((C, CH)), DMA((C, CH)),
        ],
        compiler_params=pltpu.CompilerParams(collective_id=0, has_side_effects=True, vmem_limit_bytes=56 << 20),
        cost_estimate=pl.CostEstimate(flops=2 * 1300 * 10**6, bytes_accessed=8 << 20, transcendentals=0),
    )(
        panel_parent.reshape(CH), child_inverse[0, 0], child_rhs[0, 0], panels[0, 0], panel_rows[0, 0],
        parent_inverse[0, 0], parent_rhs[0, 0],
    )
    return child[None, None], parent[None, None]


def solution(mesh):
    placed = (
        P("prow", "pcol", None, None, None),
        P("prow", "pcol", None, None, None),
        P("prow", "pcol", None, None, None),
        P("prow", "pcol", None, None),
        P("prow", "pcol", None, None),
        P("prow", "pcol", None, None),
        P("prow", "pcol", None, None),
    )
    return jax.shard_map(
        body,
        mesh=mesh,
        in_specs=placed,
        out_specs=(P("prow", "pcol", None, None, None), P("prow", "pcol", None, None)),
        check_vma=False,
    )
```

```python
import jax
import jax.numpy as jnp
from jax import lax
from jax.experimental import pallas as pl
from jax.experimental.pallas import tpu as pltpu
from jax.sharding import PartitionSpec as P

MESH = pl.DeviceIdType.MESH
F32 = jnp.float32
BF16 = jnp.bfloat16
DMA = pltpu.SemaphoreType.DMA
W = 256
R = 128
CH = 8
C = 4
CW = 64

SCRATCH = dict(
    inverse=pltpu.VMEM((CH, W, W), F32),
    rhs=pltpu.VMEM((CH, W, W), F32),
    panels=pltpu.VMEM((CH, R, W), F32),
    panel_high=pltpu.VMEM((CH, R, W), BF16),
    panel_low=pltpu.VMEM((CH, R, W), BF16),
    y_send=pltpu.VMEM((C, CH, CW, W), F32),
    y_in=pltpu.VMEM((C, CH, CW, W), F32),
    update=pltpu.VMEM((CH, CW, R), F32),
    rows_send=pltpu.VMEM((2, 4, 8, R), jnp.int32),
    rows_in=pltpu.VMEM((2, 4, 8, R), jnp.int32),
    one_hot=pltpu.VMEM((2, 2, W, 4 * R), BF16),
    first_send=pltpu.VMEM((C, 2, 4, 2, CW, R), F32),
    first_in=pltpu.VMEM((C, 2, 4, 2, CW, R), F32),
    dense=pltpu.VMEM((C, 2, 2, CW, W), F32),
    second_in=pltpu.VMEM((C, 4, CW, W), F32),
    k_high=pltpu.VMEM((W, W), BF16),
    k_low=pltpu.VMEM((W, W), BF16),
    z_parent=pltpu.VMEM((W, W), F32),
    x_block=pltpu.VMEM((C, 2, 2, CW, W), F32),
    x_all=pltpu.VMEM((W, W), F32),
    pick_send=pltpu.VMEM((C, 2, 4, 2, CW, R), F32),
    pick_in_0=pltpu.VMEM((2, 4, 2, CW, R), F32),
    pick_in_1=pltpu.VMEM((2, 4, 2, CW, R), F32),
    pick_in_2=pltpu.VMEM((2, 4, 2, CW, R), F32),
    pick_in_3=pltpu.VMEM((2, 4, 2, CW, R), F32),
    v_send=pltpu.VMEM((C, CH, CW, R), F32),
    v_in=pltpu.VMEM((C, CH, CW, R), F32),
    panel_in=pltpu.VMEM((CH, R, W), F32),
    gain_high=pltpu.VMEM((CH, R, W), BF16),
    gain_low=pltpu.VMEM((CH, R, W), BF16),
    z_child=pltpu.VMEM((CH, W, W), F32),
    out_buf=pltpu.VMEM((CH, W, W), F32),
    load_sem=DMA((3, CH)),
    out_sem=DMA((2, CH)),
    y_s=DMA((C, CH)), y_r=DMA((C, CH)),
    p_s=DMA((CH,)), p_r=DMA((CH,)),
    i_s=DMA((2, 4)), i_r=DMA((2, 4)),
    s1_s=DMA((C, 2, 4)), s1_r=DMA((C, 2, 4)),
    s2_s=DMA((C, 3)), s2_r=DMA((C, 4)),
    t1_s=DMA((C, 4)), t1_r=DMA((C, 2, 2)),
    t2_s=DMA((C, 2, 4)), t2_r=DMA((C, 2, 4)),
    v_s=DMA((C, CH)), v_r=DMA((C, CH)),
)
NN = ((1,), (0,))
NT = ((1,), (1,))
TN = ((0,), (0,))


def split(value):
    high = value.astype(BF16)
    low = (value - high.astype(F32)).astype(BF16)
    return high, low


def dot(a, b, dims=NN):
    return lax.dot_general(a, b, (dims, ((), ())), preferred_element_type=F32)


def product(a, b, dims=NN):
    a_high, a_low = split(a)
    b_high, b_low = split(b)
    return dot(a_high, b_high, dims) + (dot(a_high, b_low, dims) + dot(a_low, b_high, dims))


def streamed(a, b_high, b_low, dims=NN):
    rows = a.shape[0]
    a_high, a_low = split(a)
    both = dot(jnp.concatenate([a_high, a_low], axis=0), b_high, dims)
    return both[:rows] + (both[rows:] + dot(a_high, b_low, dims))


def chosen(a, one_hot, dims=NN):
    rows = a.shape[0]
    a_high, a_low = split(a)
    both = dot(jnp.concatenate([a_high, a_low], axis=0), one_hot, dims)
    return both[:rows] + both[rows:]


def kernel(parent_ids, inverse_hbm, rhs_hbm, panels_hbm, rows_ref, pinv_ref, prhs_ref, child_out, parent_out, *scratch):
    ref = dict(zip(SCRATCH, scratch))
    inverse, rhs, panels, panel_high, panel_low = (ref[n] for n in ("inverse", "rhs", "panels", "panel_high", "panel_low"))
    y_send, y_in, update, rows_send, rows_in = (ref[n] for n in ("y_send", "y_in", "update", "rows_send", "rows_in"))
    one_hot, first_send, first_in, dense, second_in = (ref[n] for n in ("one_hot", "first_send", "first_in", "dense", "second_in"))
    k_high, k_low, z_parent, x_block, x_all = (ref[n] for n in ("k_high", "k_low", "z_parent", "x_block", "x_all"))
    pick_send, v_send, v_in, panel_in = (ref[n] for n in ("pick_send", "v_send", "v_in", "panel_in"))
    pick_in = [ref["pick_in_%d" % c] for c in range(C)]
    gain_high, gain_low, z_child, out_buf = (ref[n] for n in ("gain_high", "gain_low", "z_child", "out_buf"))
    load_sem, out_sem, y_s, y_r, p_s, p_r, i_s, i_r = (ref[n] for n in ("load_sem", "out_sem", "y_s", "y_r", "p_s", "p_r", "i_s", "i_r"))
    s1_s, s1_r, s2_s, s2_r, t1_s, t1_r = (ref[n] for n in ("s1_s", "s1_r", "s2_s", "s2_r", "t1_s", "t1_r"))
    t2_s, t2_r, v_s, v_r = (ref[n] for n in ("t2_s", "t2_r", "v_s", "v_r"))

    r = lax.axis_index("prow")
    q = lax.axis_index("pcol")
    z, core = r // 2, r % 2
    x, y = q // 4, q % 4
    cls = (x + y + core) % 2
    own_pos = jnp.where(cls == 0, y, x)
    other_pos = jnp.where(cls == 0, x, y)
    t_self = own_pos // 2
    first_pos = (x, y)

    def partner(j):
        m = j // 2
        step = jnp.where(m == 0, 2, jnp.where(m == 1, 1, jnp.where(m == 2, 3, 0)))
        return ((z + step) % 4) * 2 + (core + j + m // 3) % 2

    def each(first, last, action):
        def one(j, carry):
            action(j)
            return carry

        lax.fori_loop(first, last, one, 0)

    def first_dev(f, a):
        return (r, a * 4 + y) if f == 0 else (r, x * 4 + a)

    def own_dev(a):
        return (r, jnp.where(cls == 0, x * 4 + a, a * 4 + y))

    def other_dev(a):
        return (r, jnp.where(cls == 0, a * 4 + y, x * 4 + a))

    def remote(src, dst, send, recv, dev):
        return pltpu.make_async_remote_copy(
            src_ref=src, dst_ref=dst, send_sem=send, recv_sem=recv, device_id=dev, device_id_type=MESH
        )

    barrier = pltpu.get_barrier_semaphore()
    each(0, 7, lambda j: pl.semaphore_signal(barrier, inc=1, device_id=(partner(j), q), device_id_type=MESH))
    for f in range(2):
        for d in range(1, 4):
            pl.semaphore_signal(barrier, inc=1, device_id=first_dev(f, (first_pos[f] + d) % 4), device_id_type=MESH)

    def load(k):
        return (
            pltpu.make_async_copy(inverse_hbm.at[k], inverse.at[k], load_sem.at[0, k]),
            pltpu.make_async_copy(rhs_hbm.at[k], rhs.at[k], load_sem.at[1, k]),
        )

    def start_load(j):
        for copy in load(partner(j)):
            copy.start()

    each(0, 8, start_load)
    panel_load = pltpu.make_async_copy(panels_hbm, panels, load_sem.at[2, 0])
    panel_load.start()

    def y_copy(c, k):
        return remote(y_send.at[c, k], y_in.at[c, r], y_s.at[c, k], y_r.at[c, r], (k, q))

    def y_wait(c, s):
        return remote(y_send.at[c, s], y_in.at[c, s], y_s.at[c, s], y_r.at[c, s], (s, q))

    def forward(k):
        for copy in load(k):
            copy.wait()
        value = product(inverse[k], rhs[k]).T
        for c in range(C):
            y_send[c, k] = value[c * CW:(c + 1) * CW]

    def forward_step(j):
        forward(partner(j))
        y_copy(0, partner(j)).start()

    forward(partner(0))
    pl.semaphore_wait(barrier, 13)
    y_copy(0, partner(0)).start()
    each(1, 7, forward_step)
    forward(r)
    for c in range(C):
        y_in[c, r] = y_send[c, r]

    def y_follow(c):
        each(0, 7, lambda j: y_copy(c - 1, partner(j)).wait_send())
        each(0, 7, lambda j: y_copy(c, partner(j)).start())

    def parent_of(f, a, t):
        if f == 0:
            return a * 4 + (a + core) % 2 + 2 * t
        return ((a + core + 1) % 2 + 2 * t) * 4 + a

    def rows_copy(f, a):
        return remote(rows_send.at[f, a], rows_in.at[f, first_pos[f]], i_s.at[f, a], i_r.at[f, first_pos[f]], first_dev(f, a))

    def rows_wait(f, a):
        return remote(rows_send.at[f, a], rows_in.at[f, a], i_s.at[f, a], i_r.at[f, a], first_dev(f, a))

    def send_rows():
        for f in range(2):
            for a in range(4):
                for t in range(2):
                    p = parent_of(f, a, t)
                    listed = jnp.full((1, R), -1, jnp.int32)
                    for s in range(CH):
                        listed = jnp.where(parent_ids[s] == p, rows_ref[s:s + 1, :], listed)
                    rows_send[f, a, t:t + 1, :] = listed
                rows_send[f, a, 2:8, :] = jnp.zeros((6, R), jnp.int32)
            rows_in[f, first_pos[f]] = rows_send[f, first_pos[f]]
            for d in range(1, 4):
                rows_copy(f, (first_pos[f] + d) % 4).start()

    def split_panels():
        panel_load.wait()
        for s in range(CH):
            high, low = split(panels[s])
            panel_high[s] = high
            panel_low[s] = low

    def gram():
        value = product(pinv_ref[...], pinv_ref[...], TN)
        high, low = split(value)
        k_high[...] = high
        k_low[...] = low
        z_parent[...] = product(value, prhs_ref[...]).T

    def make_one_hot():
        places = lax.broadcasted_iota(jnp.int32, (W, R), 0)
        for f in range(2):
            for d in range(1, 4):
                rows_wait(f, (first_pos[f] + d) % 4).wait_recv()
            for a in range(4):
                for t in range(2):
                    matrix = jnp.where(places == rows_in[f, a, t:t + 1, :], 1.0, 0.0)
                    one_hot[f, t, :, a * R:(a + 1) * R] = matrix.astype(BF16)

    def first_copy(c, f, a):
        return remote(first_send.at[c, f, a], first_in.at[c, f, first_pos[f]], s1_s.at[c, f, a], s1_r.at[c, f, first_pos[f]], first_dev(f, a))

    def first_wait(c, f, a):
        return remote(first_send.at[c, f, a], first_in.at[c, f, a], s1_s.at[c, f, a], s1_r.at[c, f, a], first_dev(f, a))

    def step_update(c):
        def one(s):
            update[s] = streamed(y_in[c, s], panel_high[s], panel_low[s], NT)

        def arrived(j):
            s = partner(6 - j)
            y_wait(c, s).wait_recv()
            one(s)

        one(r)
        each(0, 7, arrived)
        for f in range(2):
            for a in range(4):
                for t in range(2):
                    p = parent_of(f, a, t)
                    slot = jnp.int32(0)
                    for s in range(1, CH):
                        slot = jnp.where(parent_ids[s] == p, s, slot)
                    first_send[c, f, a, t] = update[slot]
            first_in[c, f, first_pos[f]] = first_send[c, f, first_pos[f]]
            for d in (2, 1, 3):
                first_copy(c, f, (first_pos[f] + d) % 4).start()

    def second_own(c):
        a = (own_pos + 2) % 4
        return remote(dense.at[c, cls, 1 - t_self], second_in.at[c, own_pos], s2_s.at[c, 2], s2_r.at[c, own_pos], own_dev(a))

    def second_other(c, t):
        a = (other_pos + 1) % 2 + 2 * t
        return remote(dense.at[c, 1 - cls, t], second_in.at[c, other_pos], s2_s.at[c, t], s2_r.at[c, other_pos], other_dev(a))

    def second_wait(c, a):
        return remote(dense.at[c, 0, 0], second_in.at[c, a], s2_s.at[c, 0], s2_r.at[c, a], own_dev(a))

    def step_dense(c):
        for f in range(2):
            for d in (1, 3, 2):
                first_wait(c, f, (first_pos[f] + d) % 4).wait_recv()
            for t in range(2):
                blocks = jnp.concatenate([first_in[c, f, a, t] for a in range(4)], axis=1)
                dense[c, f, t] = chosen(blocks, one_hot[f, t], NT)
        second_own(c).start()
        for t in range(2):
            second_other(c, t).start()

    def x_copy(c, d):
        return remote(x_block.at[c, cls, t_self], x_block.at[c, cls, t_self], t1_s.at[c, d], t1_r.at[c, cls, t_self], own_dev((own_pos + d) % 4))

    def x_wait_own(c):
        return remote(x_block.at[c, cls, 1 - t_self], x_block.at[c, cls, 1 - t_self], t1_s.at[c, 1], t1_r.at[c, cls, 1 - t_self], own_dev((own_pos + 2) % 4))

    def x_wait_other(c, t):
        a = (other_pos + 1) % 2 + 2 * t
        return remote(x_block.at[c, 1 - cls, t], x_block.at[c, 1 - cls, t], t1_s.at[c, 1], t1_r.at[c, 1 - cls, t], other_dev(a))

    def step_parent(c):
        total = dense[c, cls, t_self]
        for d in (1, 3, 2):
            a = (own_pos + d) % 4
            second_wait(c, a).wait_recv()
            total = total + second_in[c, a]
        value = z_parent[c * CW:(c + 1) * CW] - streamed(total, k_high[...], k_low[...])
        x_block[c, cls, t_self] = value
        for d in (2, 1, 3):
            x_copy(c, d).start()
        x_all[c * CW:(c + 1) * CW] = value

    def pick_copy(c, f, a):
        return remote(pick_send.at[c, f, a], pick_in[c].at[f, first_pos[f]], t2_s.at[c, f, a], t2_r.at[c, f, first_pos[f]], first_dev(f, a))

    def pick_wait(c, f, a):
        return remote(pick_send.at[c, f, a], pick_in[c].at[f, a], t2_s.at[c, f, a], t2_r.at[c, f, a], first_dev(f, a))

    def step_pick(c):
        for t in range(2):
            x_wait_other(c, t).wait_recv()
        x_wait_own(c).wait_recv()
        for f in range(2):
            for t in range(2):
                picked = chosen(x_block[c, f, t], one_hot[f, t])
                for a in range(4):
                    pick_send[c, f, a, t] = picked[:, a * R:(a + 1) * R]
            pick_in[c][f, first_pos[f]] = pick_send[c, f, first_pos[f]]
            for d in (2, 1, 3):
                pick_copy(c, f, (first_pos[f] + d) % 4).start()

    def v_copy(c, s):
        return remote(v_send.at[c, s], v_in.at[c, r], v_s.at[c, s], v_r.at[c, r], (s, q))

    def v_wait(c, s):
        return remote(v_send.at[c, s], v_in.at[c, s], v_s.at[c, s], v_r.at[c, s], (s, q))

    def step_return(c):
        for f in range(2):
            for d in (1, 3, 2):
                pick_wait(c, f, (first_pos[f] + d) % 4).wait_recv()

        def one(s):
            p = parent_ids[s]
            x_p, y_p = p // 4, p % 4
            f = (x_p + y_p + core) % 2
            a = jnp.where(f == 0, x_p, y_p)
            t = jnp.where(f == 0, y_p, x_p) // 2
            v_send[c, s] = pick_in[c][f, a, t]

        def go(j):
            s = partner(j)
            one(s)
            v_copy(c, s).start()

        each(0, 7, go)
        one(r)
        v_in[c, r] = v_send[c, r]

    def panel_copy(k):
        return remote(panels.at[k], panel_in.at[r], p_s.at[k], p_r.at[r], (k, q))

    def panel_wait(s):
        return remote(panels.at[s], panel_in.at[s], p_s.at[s], p_r.at[s], (s, q))

    def send_panels():
        each(0, 7, lambda j: y_copy(C - 1, partner(j)).wait_send())
        each(0, 7, lambda j: panel_copy(partner(j)).start())
        panel_in[r] = panels[r]

    def gains():
        each(0, 7, lambda j: panel_wait(partner(6 - j)).wait_recv())

        def one(s):
            high, low = split(product(panel_in[s], inverse[s]))
            gain_high[s] = high
            gain_low[s] = low

        each(0, CH, one)

    def solved():
        def one(k):
            value = jnp.concatenate([y_send[c, k] for c in range(C)], axis=0)
            z_child[k] = product(value, inverse[k])

        each(0, CH, one)

    def out_copy(h, k):
        return pltpu.make_async_copy(out_buf.at[k, :, pl.ds(h * R, R)], child_out.at[k, :, pl.ds(h * R, R)], out_sem.at[h, k])

    def step_final(c):
        def one(s):
            part = pl.ds(c * CW, CW)
            value = z_child[s, part] - streamed(v_in[c, s], gain_high[s], gain_low[s])
            if c % 2 == 0:
                z_child[s, part] = value
            else:
                both = jnp.concatenate([z_child[s, pl.ds((c - 1) * CW, CW)], value], axis=0)
                out_buf[s, :, c // 2 * R:(c // 2 + 1) * R] = both.T
                out_copy(c // 2, s).start()

        def arrived(j):
            s = partner(6 - j)
            v_wait(c, s).wait_recv()
            one(s)

        one(r)
        each(0, 7, arrived)

    send_rows()
    split_panels()
    gram()
    make_one_hot()

    y_follow(1)
    step_update(0)
    solved()
    step_dense(0)
    y_follow(2)
    step_update(1)
    step_parent(0)
    step_dense(1)
    y_follow(3)
    step_update(2)
    step_pick(0)
    step_parent(1)
    step_dense(2)
    send_panels()
    step_update(3)
    step_return(0)
    step_pick(1)
    step_parent(2)
    step_dense(3)
    step_return(1)
    step_pick(2)
    step_parent(3)
    parent_out[...] = x_all[...].T
    step_return(2)
    step_pick(3)
    gains()
    step_final(0)
    step_final(1)
    step_return(3)
    step_final(2)
    step_final(3)

    def z_done(j):
        k = partner(j)
        panel_copy(k).wait_send()
        for c in range(C):
            v_copy(c, k).wait_send()

    each(0, 7, z_done)
    for f in range(2):
        for d in range(1, 4):
            a = (first_pos[f] + d) % 4
            rows_copy(f, a).wait_send()
            for c in range(C):
                first_copy(c, f, a).wait_send()
                pick_copy(c, f, a).wait_send()
    for c in range(C):
        second_own(c).wait_send()
        for t in range(2):
            second_other(c, t).wait_send()
        for d in range(1, 4):
            x_copy(c, d).wait_send()

    def out_done(k):
        for h in range(2):
            out_copy(h, k).wait()

    each(0, CH, out_done)


def body(child_inverse, child_rhs, panels, panel_parent, panel_rows, parent_inverse, parent_rhs):
    vmem = pl.BlockSpec(memory_space=pltpu.VMEM)
    anywhere = pl.BlockSpec(memory_space=pl.ANY)
    child, parent = pl.pallas_call(
        kernel,
        out_shape=(jax.ShapeDtypeStruct((CH, W, W), F32), jax.ShapeDtypeStruct((W, W), F32)),
        in_specs=[pl.BlockSpec(memory_space=pltpu.SMEM), anywhere, anywhere, anywhere, vmem, vmem, vmem],
        out_specs=(anywhere, vmem),
        scratch_shapes=list(SCRATCH.values()),
        compiler_params=pltpu.CompilerParams(collective_id=0, has_side_effects=True, vmem_limit_bytes=56 << 20),
        cost_estimate=pl.CostEstimate(flops=2 * 2100 * 10**6, bytes_accessed=8 << 20, transcendentals=0),
    )(
        panel_parent.reshape(CH), child_inverse[0, 0], child_rhs[0, 0], panels[0, 0], panel_rows[0, 0],
        parent_inverse[0, 0], parent_rhs[0, 0],
    )
    return child[None, None], parent[None, None]


def solution(mesh):
    placed = (
        P("prow", "pcol", None, None, None),
        P("prow", "pcol", None, None, None),
        P("prow", "pcol", None, None, None),
        P("prow", "pcol", None, None),
        P("prow", "pcol", None, None),
        P("prow", "pcol", None, None),
        P("prow", "pcol", None, None),
    )
    return jax.shard_map(
        body,
        mesh=mesh,
        in_specs=placed,
        out_specs=(P("prow", "pcol", None, None, None), P("prow", "pcol", None, None)),
        check_vma=False,
    )
```

```python
import jax
import jax.numpy as jnp
from jax import lax
from jax.experimental import pallas as pl
from jax.experimental.pallas import tpu as pltpu
from jax.sharding import PartitionSpec as P

MESH = pl.DeviceIdType.MESH
F32 = jnp.float32
BF16 = jnp.bfloat16
DMA = pltpu.SemaphoreType.DMA
W = 256
R = 128
CH = 8
WIDTHS = [64, 64, 64, 64]
C = len(WIDTHS)
STARTS = [sum(WIDTHS[:c]) for c in range(C)]

SCRATCH = dict(
    inverse=pltpu.VMEM((CH, W, W), F32),
    rhs=pltpu.VMEM((CH, W, W), F32),
    panels=pltpu.VMEM((CH, R, W), F32),
    rows=pltpu.VMEM((CH, R), jnp.int32),
    pinv=pltpu.VMEM((W, W), F32),
    prhs=pltpu.VMEM((W, W), F32),
    panel_high=pltpu.VMEM((CH, R, W), BF16),
    panel_low=pltpu.VMEM((CH, R, W), BF16),
    rows_send=pltpu.VMEM((2, 4, 8, R), jnp.int32),
    rows_in=pltpu.VMEM((2, 4, 8, R), jnp.int32),
    one_hot=pltpu.VMEM((2, 2, W, 4 * R), BF16),
    k_high=pltpu.VMEM((W, W), BF16),
    k_low=pltpu.VMEM((W, W), BF16),
    z_parent=pltpu.VMEM((W, W), F32),
    x_all=pltpu.VMEM((W, W), F32),
    panel_in=pltpu.VMEM((CH, R, W), F32),
    gain_high=pltpu.VMEM((CH, R, W), BF16),
    gain_low=pltpu.VMEM((CH, R, W), BF16),
    z_child=pltpu.VMEM((CH, W, W), F32),
    out_buf=pltpu.VMEM((CH, W, W), F32),
    load_sem=DMA((3, CH)),
    out_sem=DMA((3, CH)),
    y_s=DMA((C, CH)), y_r=DMA((C, CH)),
    p_s=DMA((CH,)), p_r=DMA((CH,)),
    i_s=DMA((2, 4)), i_r=DMA((2, 4)),
    s1_s=DMA((C, 2, 4)), s1_r=DMA((C, 2, 4)),
    s2_s=DMA((C, 3)), s2_r=DMA((C, 4)),
    t1_s=DMA((C, 4)), t1_r=DMA((C, 2, 2)),
    t2_s=DMA((C, 2, 4)), t2_r=DMA((C, 2, 4)),
    v_s=DMA((C, CH)), v_r=DMA((C, CH)),
)
CHUNKED = dict(
    y_send=(CH, None, W),
    y_in=(CH, None, W),
    update=(CH, None, R),
    first_send=(2, 4, 2, None, R),
    first_in=(2, 4, 2, None, R),
    dense=(2, 2, None, W),
    second_in=(4, None, W),
    x_block=(2, 2, None, W),
    pick_send=(2, 4, 2, None, R),
    pick_in=(2, 4, 2, None, R),
    v_send=(CH, None, R),
    v_in=(CH, None, R),
)
for name, shape in CHUNKED.items():
    for c in range(C):
        SCRATCH[name + str(c)] = pltpu.VMEM(tuple(WIDTHS[c] if n is None else n for n in shape), F32)
NN = ((1,), (0,))
NT = ((1,), (1,))
TN = ((0,), (0,))

ORDER = [
    "solved", "U0", "U1", "D0", "U2", "D1", "P0", "U3", "D2", "P1",
    "K0", "D3", "P2", "K1", "gains", "R0", "P3", "parent", "K2", "F0",
    "R1", "K3", "R2", "F1", "R3", "F2", "F3",
]


def split(value):
    high = value.astype(BF16)
    low = (value - high.astype(F32)).astype(BF16)
    return high, low


def dot(a, b, dims=NN):
    return lax.dot_general(a, b, (dims, ((), ())), preferred_element_type=F32)


def product(a, b, dims=NN):
    a_high, a_low = split(a)
    b_high, b_low = split(b)
    return dot(a_high, b_high, dims) + (dot(a_high, b_low, dims) + dot(a_low, b_high, dims))


def streamed(a, b_high, b_low, dims=NN):
    rows = a.shape[0]
    a_high, a_low = split(a)
    both = dot(jnp.concatenate([a_high, a_low], axis=0), b_high, dims)
    return both[:rows] + (both[rows:] + dot(a_high, b_low, dims))


def chosen(a, one_hot, dims=NN):
    rows = a.shape[0]
    a_high, a_low = split(a)
    both = dot(jnp.concatenate([a_high, a_low], axis=0), one_hot, dims)
    return both[:rows] + both[rows:]


def kernel(parent_ids, inverse_hbm, rhs_hbm, panels_hbm, rows_hbm, pinv_hbm, prhs_hbm, child_out, parent_out, *scratch):
    ref = dict(zip(SCRATCH, scratch))
    inverse = ref["inverse"]
    rhs = ref["rhs"]
    panels = ref["panels"]
    rows = ref["rows"]
    pinv = ref["pinv"]
    prhs = ref["prhs"]
    panel_high = ref["panel_high"]
    panel_low = ref["panel_low"]
    rows_send = ref["rows_send"]
    rows_in = ref["rows_in"]
    one_hot = ref["one_hot"]
    k_high = ref["k_high"]
    k_low = ref["k_low"]
    z_parent = ref["z_parent"]
    x_all = ref["x_all"]
    panel_in = ref["panel_in"]
    gain_high = ref["gain_high"]
    gain_low = ref["gain_low"]
    z_child = ref["z_child"]
    out_buf = ref["out_buf"]
    load_sem = ref["load_sem"]
    out_sem = ref["out_sem"]
    y_s = ref["y_s"]
    y_r = ref["y_r"]
    p_s = ref["p_s"]
    p_r = ref["p_r"]
    i_s = ref["i_s"]
    i_r = ref["i_r"]
    s1_s = ref["s1_s"]
    s1_r = ref["s1_r"]
    s2_s = ref["s2_s"]
    s2_r = ref["s2_r"]
    t1_s = ref["t1_s"]
    t1_r = ref["t1_r"]
    t2_s = ref["t2_s"]
    t2_r = ref["t2_r"]
    v_s = ref["v_s"]
    v_r = ref["v_r"]
    y_send = [ref["y_send" + str(c)] for c in range(C)]
    y_in = [ref["y_in" + str(c)] for c in range(C)]
    update = [ref["update" + str(c)] for c in range(C)]
    first_send = [ref["first_send" + str(c)] for c in range(C)]
    first_in = [ref["first_in" + str(c)] for c in range(C)]
    dense = [ref["dense" + str(c)] for c in range(C)]
    second_in = [ref["second_in" + str(c)] for c in range(C)]
    x_block = [ref["x_block" + str(c)] for c in range(C)]
    pick_send = [ref["pick_send" + str(c)] for c in range(C)]
    pick_in = [ref["pick_in" + str(c)] for c in range(C)]
    v_send = [ref["v_send" + str(c)] for c in range(C)]
    v_in = [ref["v_in" + str(c)] for c in range(C)]

    r = lax.axis_index("prow")
    q = lax.axis_index("pcol")
    z, core = r // 2, r % 2
    x, y = q // 4, q % 4
    cls = (x + y + core) % 2
    own_pos = jnp.where(cls == 0, y, x)
    other_pos = jnp.where(cls == 0, x, y)
    t_self = own_pos // 2
    first_pos = (x, y)

    def partner(j):
        m = j // 2
        step = jnp.where(m == 0, 2, jnp.where(m == 1, 1, jnp.where(m == 2, 3, 0)))
        return ((z + step) % 4) * 2 + (core + j + m // 3) % 2

    def each(first, last, action, unroll=1):
        def one(j, carry):
            action(j)
            return carry

        lax.fori_loop(first, last, one, 0, unroll=unroll)

    def first_dev(f, a):
        return (r, a * 4 + y) if f == 0 else (r, x * 4 + a)

    def own_dev(a):
        return (r, jnp.where(cls == 0, x * 4 + a, a * 4 + y))

    def other_dev(a):
        return (r, jnp.where(cls == 0, a * 4 + y, x * 4 + a))

    def remote(src, dst, send, recv, dev):
        return pltpu.make_async_remote_copy(
            src_ref=src, dst_ref=dst, send_sem=send, recv_sem=recv, device_id=dev, device_id_type=MESH
        )

    barrier = pltpu.get_barrier_semaphore()
    each(0, 7, lambda j: pl.semaphore_signal(barrier, inc=1, device_id=(partner(j), q), device_id_type=MESH))
    for f in range(2):
        for d in range(1, 4):
            pl.semaphore_signal(barrier, inc=1, device_id=first_dev(f, (first_pos[f] + d) % 4), device_id_type=MESH)

    def load(k):
        return (
            pltpu.make_async_copy(inverse_hbm.at[k], inverse.at[k], load_sem.at[0, k]),
            pltpu.make_async_copy(rhs_hbm.at[k], rhs.at[k], load_sem.at[1, k]),
        )

    def start_load(j):
        for copy in load(partner(j)):
            copy.start()

    each(0, 8, start_load)
    panel_load = pltpu.make_async_copy(panels_hbm, panels, load_sem.at[2, 0])
    rows_load = pltpu.make_async_copy(rows_hbm, rows, load_sem.at[2, 1])
    pinv_load = pltpu.make_async_copy(pinv_hbm, pinv, load_sem.at[2, 2])
    prhs_load = pltpu.make_async_copy(prhs_hbm, prhs, load_sem.at[2, 3])
    for copy in (rows_load, panel_load, pinv_load, prhs_load):
        copy.start()

    def y_copy(c, k):
        return remote(y_send[c].at[k], y_in[c].at[r], y_s.at[c, k], y_r.at[c, r], (k, q))

    def y_wait(c, s):
        return remote(y_send[c].at[s], y_in[c].at[s], y_s.at[c, s], y_r.at[c, s], (s, q))

    def forward(k):
        for copy in load(k):
            copy.wait()
        value = product(inverse[k], rhs[k]).T
        for c in range(C):
            y_send[c][k] = value[STARTS[c]:STARTS[c] + WIDTHS[c]]

    def forward_step(j):
        forward(partner(j))
        y_copy(0, partner(j)).start()

    forward(partner(0))
    pl.semaphore_wait(barrier, 13)
    y_copy(0, partner(0)).start()
    each(1, 7, forward_step)
    forward(r)
    for c in range(C):
        y_in[c][r] = y_send[c][r]

    def y_follow(c):
        each(0, 7, lambda j: y_copy(c, partner(j)).start())

    def parent_of(f, a, t):
        if f == 0:
            return a * 4 + (a + core) % 2 + 2 * t
        return ((a + core + 1) % 2 + 2 * t) * 4 + a

    def rows_copy(f, a):
        return remote(rows_send.at[f, a], rows_in.at[f, first_pos[f]], i_s.at[f, a], i_r.at[f, first_pos[f]], first_dev(f, a))

    def rows_wait(f, a):
        return remote(rows_send.at[f, a], rows_in.at[f, a], i_s.at[f, a], i_r.at[f, a], first_dev(f, a))

    def send_rows():
        rows_load.wait()
        for f in range(2):
            for a in range(4):
                for t in range(2):
                    p = parent_of(f, a, t)
                    listed = jnp.full((1, R), -1, jnp.int32)
                    for s in range(CH):
                        listed = jnp.where(parent_ids[s] == p, rows[s:s + 1, :], listed)
                    rows_send[f, a, t:t + 1, :] = listed
                rows_send[f, a, 2:8, :] = jnp.zeros((6, R), jnp.int32)
            rows_in[f, first_pos[f]] = rows_send[f, first_pos[f]]
            for d in range(1, 4):
                rows_copy(f, (first_pos[f] + d) % 4).start()

    def split_panels():
        panel_load.wait()
        for s in range(CH):
            high, low = split(panels[s])
            panel_high[s] = high
            panel_low[s] = low

    def gram():
        pinv_load.wait()
        prhs_load.wait()
        value = product(pinv[...], pinv[...], TN)
        high, low = split(value)
        k_high[...] = high
        k_low[...] = low
        z_parent[...] = product(value, prhs[...]).T

    def make_one_hot():
        places = lax.broadcasted_iota(jnp.int32, (W, R), 0)
        for f in range(2):
            for d in range(1, 4):
                rows_wait(f, (first_pos[f] + d) % 4).wait_recv()
            for a in range(4):
                for t in range(2):
                    matrix = jnp.where(places == rows_in[f, a, t:t + 1, :], 1.0, 0.0)
                    one_hot[f, t, :, a * R:(a + 1) * R] = matrix.astype(BF16)

    def first_copy(c, f, a):
        return remote(first_send[c].at[f, a], first_in[c].at[f, first_pos[f]], s1_s.at[c, f, a], s1_r.at[c, f, first_pos[f]], first_dev(f, a))

    def first_wait(c, f, a):
        return remote(first_send[c].at[f, a], first_in[c].at[f, a], s1_s.at[c, f, a], s1_r.at[c, f, a], first_dev(f, a))

    def step_update(c):
        def one(s):
            update[c][s] = streamed(y_in[c][s], panel_high[s], panel_low[s], NT)

        each(0, 5, lambda j: y_wait(c, partner(6 - j)).wait_recv())
        each(0, 6, lambda j: one(partner(7 - j)), 6)
        each(0, 2, lambda j: y_wait(c, partner(j)).wait_recv())
        each(0, 2, lambda j: one(partner(j)), 2)
        for f in range(2):
            for a in range(4):
                for t in range(2):
                    p = parent_of(f, a, t)
                    slot = jnp.int32(0)
                    for s in range(1, CH):
                        slot = jnp.where(parent_ids[s] == p, s, slot)
                    first_send[c][f, a, t] = update[c][slot]
            first_in[c][f, first_pos[f]] = first_send[c][f, first_pos[f]]
            for d in (2, 1, 3):
                first_copy(c, f, (first_pos[f] + d) % 4).start()

    def second_own(c):
        a = (own_pos + 2) % 4
        return remote(dense[c].at[cls, 1 - t_self], second_in[c].at[own_pos], s2_s.at[c, 2], s2_r.at[c, own_pos], own_dev(a))

    def second_other(c, t):
        a = (other_pos + 1) % 2 + 2 * t
        return remote(dense[c].at[1 - cls, t], second_in[c].at[other_pos], s2_s.at[c, t], s2_r.at[c, other_pos], other_dev(a))

    def second_wait(c, a):
        return remote(dense[c].at[0, 0], second_in[c].at[a], s2_s.at[c, 0], s2_r.at[c, a], own_dev(a))

    def step_dense(c):
        for f in range(2):
            for d in (1, 3, 2):
                first_wait(c, f, (first_pos[f] + d) % 4).wait_recv()
            for t in range(2):
                blocks = jnp.concatenate([first_in[c][f, a, t] for a in range(4)], axis=1)
                dense[c][f, t] = chosen(blocks, one_hot[f, t], NT)
        second_own(c).start()
        for t in range(2):
            second_other(c, t).start()

    def x_copy(c, d):
        return remote(x_block[c].at[cls, t_self], x_block[c].at[cls, t_self], t1_s.at[c, d], t1_r.at[c, cls, t_self], own_dev((own_pos + d) % 4))

    def x_wait_own(c):
        return remote(x_block[c].at[cls, 1 - t_self], x_block[c].at[cls, 1 - t_self], t1_s.at[c, 1], t1_r.at[c, cls, 1 - t_self], own_dev((own_pos + 2) % 4))

    def x_wait_other(c, t):
        a = (other_pos + 1) % 2 + 2 * t
        return remote(x_block[c].at[1 - cls, t], x_block[c].at[1 - cls, t], t1_s.at[c, 1], t1_r.at[c, 1 - cls, t], other_dev(a))

    def step_parent(c):
        total = dense[c][cls, t_self]
        for d in (1, 3, 2):
            a = (own_pos + d) % 4
            second_wait(c, a).wait_recv()
            total = total + second_in[c][a]
        value = z_parent[STARTS[c]:STARTS[c] + WIDTHS[c]] - streamed(total, k_high[...], k_low[...])
        x_block[c][cls, t_self] = value
        for d in (2, 1, 3):
            x_copy(c, d).start()
        x_all[STARTS[c]:STARTS[c] + WIDTHS[c]] = value

    def pick_copy(c, f, a):
        return remote(pick_send[c].at[f, a], pick_in[c].at[f, first_pos[f]], t2_s.at[c, f, a], t2_r.at[c, f, first_pos[f]], first_dev(f, a))

    def pick_wait(c, f, a):
        return remote(pick_send[c].at[f, a], pick_in[c].at[f, a], t2_s.at[c, f, a], t2_r.at[c, f, a], first_dev(f, a))

    def step_pick(c):
        for t in range(2):
            x_wait_other(c, t).wait_recv()
        x_wait_own(c).wait_recv()
        for f in range(2):
            for t in range(2):
                picked = chosen(x_block[c][f, t], one_hot[f, t])
                for a in range(4):
                    pick_send[c][f, a, t] = picked[:, a * R:(a + 1) * R]
            pick_in[c][f, first_pos[f]] = pick_send[c][f, first_pos[f]]
            for d in (2, 1, 3):
                pick_copy(c, f, (first_pos[f] + d) % 4).start()

    def v_copy(c, s):
        return remote(v_send[c].at[s], v_in[c].at[r], v_s.at[c, s], v_r.at[c, r], (s, q))

    def v_wait(c, s):
        return remote(v_send[c].at[s], v_in[c].at[s], v_s.at[c, s], v_r.at[c, s], (s, q))

    def step_return(c):
        for f in range(2):
            for d in (1, 3, 2):
                pick_wait(c, f, (first_pos[f] + d) % 4).wait_recv()

        def one(s):
            p = parent_ids[s]
            x_p, y_p = p // 4, p % 4
            f = (x_p + y_p + core) % 2
            a = jnp.where(f == 0, x_p, y_p)
            t = jnp.where(f == 0, y_p, x_p) // 2
            v_send[c][s] = pick_in[c][f, a, t]

        def go(j):
            s = partner(j)
            one(s)
            v_copy(c, s).start()

        each(0, 7, go)
        one(r)
        v_in[c][r] = v_send[c][r]

    def panel_copy(k):
        return remote(panels.at[k], panel_in.at[r], p_s.at[k], p_r.at[r], (k, q))

    def panel_wait(s):
        return remote(panels.at[s], panel_in.at[s], p_s.at[s], p_r.at[s], (s, q))

    def send_panels():
        each(0, 7, lambda j: panel_copy(partner(j)).start())
        panel_in[r] = panels[r]

    def gains():
        each(0, 7, lambda j: panel_wait(partner(6 - j)).wait_recv())

        def one(s):
            high, low = split(product(panel_in[s], inverse[s]))
            gain_high[s] = high
            gain_low[s] = low

        each(0, CH, one, 4)

    def solved():
        def one(k):
            value = jnp.concatenate([y_send[c][k] for c in range(C)], axis=0)
            z_child[k] = product(value, inverse[k])

        each(0, CH, one, 4)

    def out_copy(h, k):
        return pltpu.make_async_copy(out_buf.at[k, :, pl.ds(h * R, R)], child_out.at[k, :, pl.ds(h * R, R)], out_sem.at[h, k])

    def step_final(c):
        start = STARTS[c]
        end = start + WIDTHS[c]
        half = start // R

        def one(s):
            value = z_child[s, start:end] - streamed(v_in[c][s], gain_high[s], gain_low[s])
            if end % R:
                z_child[s, start:end] = value
            else:
                if start % R:
                    value = jnp.concatenate([z_child[s, half * R:start], value], axis=0)
                out_buf[s, :, half * R:(half + 1) * R] = value.T
                out_copy(half, s).start()

        each(0, 5, lambda j: v_wait(c, partner(6 - j)).wait_recv())
        each(0, 6, lambda j: one(partner(7 - j)), 6)
        each(0, 2, lambda j: v_wait(c, partner(j)).wait_recv())
        each(0, 2, lambda j: one(partner(j)), 2)

    x_out = pltpu.make_async_copy(x_all, parent_out, out_sem.at[2, 0])

    def parent_result():
        x_all[...] = x_all[...].T
        x_out.start()

    steps = dict(U=step_update, D=step_dense, P=step_parent, K=step_pick, R=step_return, F=step_final)
    send_rows()
    for c in range(1, C):
        y_follow(c)
    split_panels()
    send_panels()
    gram()
    make_one_hot()
    for step in ORDER:
        if step == "solved":
            solved()
        elif step == "gains":
            gains()
        elif step == "parent":
            parent_result()
        else:
            steps[step[0]](int(step[1:]))

    def z_done(j):
        k = partner(j)
        panel_copy(k).wait_send()
        for c in range(C):
            y_copy(c, k).wait_send()
        for c in range(C):
            v_copy(c, k).wait_send()

    each(0, 7, z_done)
    for f in range(2):
        for d in range(1, 4):
            a = (first_pos[f] + d) % 4
            rows_copy(f, a).wait_send()
            for c in range(C):
                first_copy(c, f, a).wait_send()
                pick_copy(c, f, a).wait_send()
    for c in range(C):
        second_own(c).wait_send()
        for t in range(2):
            second_other(c, t).wait_send()
        for d in range(1, 4):
            x_copy(c, d).wait_send()

    def out_done(k):
        for h in range(2):
            out_copy(h, k).wait()

    each(0, CH, out_done)
    x_out.wait()


def body(child_inverse, child_rhs, panels, panel_parent, panel_rows, parent_inverse, parent_rhs):
    anywhere = pl.BlockSpec(memory_space=pl.ANY)
    child, parent = pl.pallas_call(
        kernel,
        out_shape=(jax.ShapeDtypeStruct((CH, W, W), F32), jax.ShapeDtypeStruct((W, W), F32)),
        in_specs=[pl.BlockSpec(memory_space=pltpu.SMEM)] + [anywhere] * 6,
        out_specs=(anywhere, anywhere),
        scratch_shapes=list(SCRATCH.values()),
        compiler_params=pltpu.CompilerParams(collective_id=0, has_side_effects=True, vmem_limit_bytes=56 << 20),
        cost_estimate=pl.CostEstimate(flops=2 * 2100 * 10**6, bytes_accessed=8 << 20, transcendentals=0),
    )(
        panel_parent.reshape(CH), child_inverse[0, 0], child_rhs[0, 0], panels[0, 0], panel_rows[0, 0],
        parent_inverse[0, 0], parent_rhs[0, 0],
    )
    return child[None, None], parent[None, None]


def solution(mesh):
    placed = (
        P("prow", "pcol", None, None, None),
        P("prow", "pcol", None, None, None),
        P("prow", "pcol", None, None, None),
        P("prow", "pcol", None, None),
        P("prow", "pcol", None, None),
        P("prow", "pcol", None, None),
        P("prow", "pcol", None, None),
    )
    return jax.shard_map(
        body,
        mesh=mesh,
        in_specs=placed,
        out_specs=(P("prow", "pcol", None, None, None), P("prow", "pcol", None, None)),
        check_vma=False,
    )
```

```python
import jax
import jax.numpy as jnp
from jax import lax
from jax.experimental import pallas as pl
from jax.experimental.pallas import tpu as pltpu
from jax.sharding import PartitionSpec as P

MESH = pl.DeviceIdType.MESH
F32 = jnp.float32
BF16 = jnp.bfloat16
DMA = pltpu.SemaphoreType.DMA
W = 256
R = 128
CH = 8
WIDTHS = [32, 32, 64, 64, 32, 32]
C = len(WIDTHS)
STARTS = [sum(WIDTHS[:c]) for c in range(C)]

SCRATCH = dict(
    inverse=pltpu.VMEM((CH, W, W), F32),
    rhs=pltpu.VMEM((CH, W, W), F32),
    panels=pltpu.VMEM((CH, R, W), F32),
    rows=pltpu.VMEM((CH, R), jnp.int32),
    pinv=pltpu.VMEM((W, W), F32),
    prhs=pltpu.VMEM((W, W), F32),
    panel_high=pltpu.VMEM((CH, R, W), BF16),
    panel_low=pltpu.VMEM((CH, R, W), BF16),
    rows_send=pltpu.VMEM((2, 4, 8, R), jnp.int32),
    rows_in=pltpu.VMEM((2, 4, 8, R), jnp.int32),
    one_hot=pltpu.VMEM((2, 2, W, 4 * R), BF16),
    k_high=pltpu.VMEM((W, W), BF16),
    k_low=pltpu.VMEM((W, W), BF16),
    z_parent=pltpu.VMEM((W, W), F32),
    x_all=pltpu.VMEM((W, W), F32),
    panel_in=pltpu.VMEM((CH, R, W), F32),
    gain_high=pltpu.VMEM((CH, R, W), BF16),
    gain_low=pltpu.VMEM((CH, R, W), BF16),
    z_child=pltpu.VMEM((CH, W, W), F32),
    out_buf=pltpu.VMEM((CH, W, W), F32),
    load_sem=DMA((3, CH)),
    out_sem=DMA((3, CH)),
    y_s=DMA((C,)), y_r=DMA((C, 2)),
    p_s=DMA((1,)), p_r=DMA((1,)),
    i_s=DMA((2,)), i_r=DMA((2,)),
    s1_s=DMA((C, 2)), s1_r=DMA((C, 2)),
    s2_s=DMA((C,)), s2_r=DMA((C,)),
    t1_s=DMA((C,)), t1_r=DMA((C,)),
    t2_s=DMA((C, 2)), t2_r=DMA((C, 2)),
    v_s=DMA((C,)), v_r=DMA((C, 2)),
)
CHUNKED = dict(
    y_send=(CH, None, W),
    y_in=(CH, None, W),
    update=(CH, None, R),
    first_send=(2, 4, 2, None, R),
    first_in=(2, 4, 2, None, R),
    dense=(2, 2, None, W),
    second_in=(4, None, W),
    x_block=(2, 2, None, W),
    pick_send=(2, 4, 2, None, R),
    pick_in=(2, 4, 2, None, R),
    v_send=(CH, None, R),
    v_in=(CH, None, R),
)
for name, shape in CHUNKED.items():
    for c in range(C):
        SCRATCH[name + str(c)] = pltpu.VMEM(tuple(WIDTHS[c] if n is None else n for n in shape), F32)
NN = ((1,), (0,))
NT = ((1,), (1,))
TN = ((0,), (0,))

ORDER = [
    "solved", "U0", "U1", "D0", "D1", "P0", "U2", "P1", "K0", "U3",
    "D2", "K1", "R0", "U4", "U5", "D3", "P2", "R1", "D4", "D5",
    "P3", "K2", "P4", "gains", "P5", "parent", "K3", "F0", "F1", "R2",
    "K4", "K5", "R3", "F2", "R4", "R5", "sent", "F3", "F4", "F5",
]


def split(value):
    high = value.astype(BF16)
    low = (value - high.astype(F32)).astype(BF16)
    return high, low


def dot(a, b, dims=NN):
    return lax.dot_general(a, b, (dims, ((), ())), preferred_element_type=F32)


def product(a, b, dims=NN):
    a_high, a_low = split(a)
    b_high, b_low = split(b)
    return dot(a_high, b_high, dims) + (dot(a_high, b_low, dims) + dot(a_low, b_high, dims))


def streamed(a, b_high, b_low, dims=NN):
    rows = a.shape[0]
    a_high, a_low = split(a)
    both = dot(jnp.concatenate([a_high, a_low], axis=0), b_high, dims)
    return both[:rows] + (both[rows:] + dot(a_high, b_low, dims))


def chosen(a, one_hot, dims=NN):
    rows = a.shape[0]
    a_high, a_low = split(a)
    both = dot(jnp.concatenate([a_high, a_low], axis=0), one_hot, dims)
    return both[:rows] + both[rows:]


def kernel(parent_ids, inverse_hbm, rhs_hbm, panels_hbm, rows_hbm, pinv_hbm, prhs_hbm, child_out, parent_out, *scratch):
    ref = dict(zip(SCRATCH, scratch))
    inverse = ref["inverse"]
    rhs = ref["rhs"]
    panels = ref["panels"]
    rows = ref["rows"]
    pinv = ref["pinv"]
    prhs = ref["prhs"]
    panel_high = ref["panel_high"]
    panel_low = ref["panel_low"]
    rows_send = ref["rows_send"]
    rows_in = ref["rows_in"]
    one_hot = ref["one_hot"]
    k_high = ref["k_high"]
    k_low = ref["k_low"]
    z_parent = ref["z_parent"]
    x_all = ref["x_all"]
    panel_in = ref["panel_in"]
    gain_high = ref["gain_high"]
    gain_low = ref["gain_low"]
    z_child = ref["z_child"]
    out_buf = ref["out_buf"]
    load_sem = ref["load_sem"]
    out_sem = ref["out_sem"]
    y_s = ref["y_s"]
    y_r = ref["y_r"]
    p_s = ref["p_s"]
    p_r = ref["p_r"]
    i_s = ref["i_s"]
    i_r = ref["i_r"]
    s1_s = ref["s1_s"]
    s1_r = ref["s1_r"]
    s2_s = ref["s2_s"]
    s2_r = ref["s2_r"]
    t1_s = ref["t1_s"]
    t1_r = ref["t1_r"]
    t2_s = ref["t2_s"]
    t2_r = ref["t2_r"]
    v_s = ref["v_s"]
    v_r = ref["v_r"]
    y_send = [ref["y_send" + str(c)] for c in range(C)]
    y_in = [ref["y_in" + str(c)] for c in range(C)]
    update = [ref["update" + str(c)] for c in range(C)]
    first_send = [ref["first_send" + str(c)] for c in range(C)]
    first_in = [ref["first_in" + str(c)] for c in range(C)]
    dense = [ref["dense" + str(c)] for c in range(C)]
    second_in = [ref["second_in" + str(c)] for c in range(C)]
    x_block = [ref["x_block" + str(c)] for c in range(C)]
    pick_send = [ref["pick_send" + str(c)] for c in range(C)]
    pick_in = [ref["pick_in" + str(c)] for c in range(C)]
    v_send = [ref["v_send" + str(c)] for c in range(C)]
    v_in = [ref["v_in" + str(c)] for c in range(C)]

    r = lax.axis_index("prow")
    q = lax.axis_index("pcol")
    z, core = r // 2, r % 2
    x, y = q // 4, q % 4
    cls = (x + y + core) % 2
    own_pos = jnp.where(cls == 0, y, x)
    other_pos = jnp.where(cls == 0, x, y)
    t_self = own_pos // 2
    first_pos = (x, y)

    partners = [((z + step) % 4) * 2 + (core + d) % 2 for step, d in ((2, 0), (2, 1), (1, 0), (1, 1), (3, 0), (3, 1), (0, 1), (0, 0))]
    far, near = partners[:2], partners[2:7]

    def first_dev(f, a):
        return (r, a * 4 + y) if f == 0 else (r, x * 4 + a)

    def own_dev(a):
        return (r, jnp.where(cls == 0, x * 4 + a, a * 4 + y))

    def other_dev(a):
        return (r, jnp.where(cls == 0, a * 4 + y, x * 4 + a))

    def remote(src, dst, send, recv, dev):
        return pltpu.make_async_remote_copy(
            src_ref=src, dst_ref=dst, send_sem=send, recv_sem=recv, device_id=dev, device_id_type=MESH
        )

    barrier = pltpu.get_barrier_semaphore()
    for k in partners[:7]:
        pl.semaphore_signal(barrier, inc=1, device_id=(k, q), device_id_type=MESH)
    for f in range(2):
        for d in range(1, 4):
            pl.semaphore_signal(barrier, inc=1, device_id=first_dev(f, (first_pos[f] + d) % 4), device_id_type=MESH)

    def load(k):
        return (
            pltpu.make_async_copy(inverse_hbm.at[k], inverse.at[k], load_sem.at[0, k]),
            pltpu.make_async_copy(rhs_hbm.at[k], rhs.at[k], load_sem.at[1, k]),
        )

    for k in partners:
        for copy in load(k):
            copy.start()
    panel_load = pltpu.make_async_copy(panels_hbm, panels, load_sem.at[2, 0])
    rows_load = pltpu.make_async_copy(rows_hbm, rows, load_sem.at[2, 1])
    pinv_load = pltpu.make_async_copy(pinv_hbm, pinv, load_sem.at[2, 2])
    prhs_load = pltpu.make_async_copy(prhs_hbm, prhs, load_sem.at[2, 3])
    for copy in (rows_load, panel_load, pinv_load, prhs_load):
        copy.start()

    def group(j):
        return 0 if j < 2 else 1

    def y_start(c, j):
        k = partners[j]
        remote(y_send[c].at[k], y_in[c].at[r], y_s.at[c], y_r.at[c, group(j)], (k, q)).start()

    def y_wait(c, g):
        blocks = y_in[c].at[pl.ds(0, (2, 5)[g])]
        remote(blocks, blocks, y_s.at[c], y_r.at[c, g], (far[0], q)).wait_recv()

    def forward(k):
        for copy in load(k):
            copy.wait()
        value = product(inverse[k], rhs[k]).T
        for c in range(C):
            y_send[c][k] = value[STARTS[c]:STARTS[c] + WIDTHS[c]]

    forward(partners[0])
    pl.semaphore_wait(barrier, 13)
    y_start(0, 0)
    for j in range(1, 7):
        forward(partners[j])
        y_start(0, j)
    forward(r)
    for c in range(C):
        y_in[c][r] = y_send[c][r]

    def y_follow(c):
        for j in range(7):
            y_start(c, j)

    def parent_of(f, a, t):
        if f == 0:
            return a * 4 + (a + core) % 2 + 2 * t
        return ((a + core + 1) % 2 + 2 * t) * 4 + a

    def rows_copy(f, a):
        return remote(rows_send.at[f, a], rows_in.at[f, first_pos[f]], i_s.at[f], i_r.at[f], first_dev(f, a))

    def rows_wait(f):
        blocks = rows_in.at[f, pl.ds(0, 3)]
        return remote(blocks, blocks, i_s.at[f], i_r.at[f], first_dev(f, (first_pos[f] + 1) % 4))

    def send_rows():
        rows_load.wait()
        for f in range(2):
            for a in range(4):
                for t in range(2):
                    p = parent_of(f, a, t)
                    listed = jnp.full((1, R), -1, jnp.int32)
                    for s in range(CH):
                        listed = jnp.where(parent_ids[s] == p, rows[s:s + 1, :], listed)
                    rows_send[f, a, t:t + 1, :] = listed
                rows_send[f, a, 2:8, :] = jnp.zeros((6, R), jnp.int32)
            rows_in[f, first_pos[f]] = rows_send[f, first_pos[f]]
            for d in range(1, 4):
                rows_copy(f, (first_pos[f] + d) % 4).start()

    def split_panels():
        panel_load.wait()
        for s in range(CH):
            high, low = split(panels[s])
            panel_high[s] = high
            panel_low[s] = low

    def gram():
        pinv_load.wait()
        prhs_load.wait()
        value = product(pinv[...], pinv[...], TN)
        high, low = split(value)
        k_high[...] = high
        k_low[...] = low
        z_parent[...] = product(value, prhs[...]).T

    def make_one_hot():
        places = lax.broadcasted_iota(jnp.int32, (W, R), 0)
        for f in range(2):
            rows_wait(f).wait_recv()
            for a in range(4):
                for t in range(2):
                    matrix = jnp.where(places == rows_in[f, a, t:t + 1, :], 1.0, 0.0)
                    one_hot[f, t, :, a * R:(a + 1) * R] = matrix.astype(BF16)

    def first_copy(c, f, a):
        return remote(first_send[c].at[f, a], first_in[c].at[f, first_pos[f]], s1_s.at[c, f], s1_r.at[c, f], first_dev(f, a))

    def first_wait(c, f):
        blocks = first_in[c].at[f, pl.ds(0, 3)]
        return remote(blocks, blocks, s1_s.at[c, f], s1_r.at[c, f], first_dev(f, (first_pos[f] + 1) % 4))

    def step_update(c):
        def one(s):
            update[c][s] = streamed(y_in[c][s], panel_high[s], panel_low[s], NT)

        y_wait(c, 1)
        for s in partners[2:]:
            one(s)
        y_wait(c, 0)
        for s in far:
            one(s)
        for f in range(2):
            for a in range(4):
                for t in range(2):
                    p = parent_of(f, a, t)
                    slot = jnp.int32(0)
                    for s in range(1, CH):
                        slot = jnp.where(parent_ids[s] == p, s, slot)
                    first_send[c][f, a, t] = update[c][slot]
            first_in[c][f, first_pos[f]] = first_send[c][f, first_pos[f]]
            for d in (2, 1, 3):
                first_copy(c, f, (first_pos[f] + d) % 4).start()

    def second_own(c):
        a = (own_pos + 2) % 4
        return remote(dense[c].at[cls, 1 - t_self], second_in[c].at[own_pos], s2_s.at[c], s2_r.at[c], own_dev(a))

    def second_other(c, t):
        a = (other_pos + 1) % 2 + 2 * t
        return remote(dense[c].at[1 - cls, t], second_in[c].at[other_pos], s2_s.at[c], s2_r.at[c], other_dev(a))

    def second_wait(c):
        blocks = second_in[c].at[pl.ds(0, 3)]
        return remote(blocks, blocks, s2_s.at[c], s2_r.at[c], own_dev((own_pos + 1) % 4))

    def step_dense(c):
        for f in range(2):
            first_wait(c, f).wait_recv()
            for t in range(2):
                blocks = jnp.concatenate([first_in[c][f, a, t] for a in range(4)], axis=1)
                dense[c][f, t] = chosen(blocks, one_hot[f, t], NT)
        second_own(c).start()
        for t in range(2):
            second_other(c, t).start()

    def x_copy(c, d):
        return remote(x_block[c].at[cls, t_self], x_block[c].at[cls, t_self], t1_s.at[c], t1_r.at[c], own_dev((own_pos + d) % 4))

    def x_wait(c):
        blocks = second_in[c].at[pl.ds(0, 3)]
        return remote(blocks, blocks, t1_s.at[c], t1_r.at[c], own_dev((own_pos + 1) % 4))

    def step_parent(c):
        total = dense[c][cls, t_self]
        second_wait(c).wait_recv()
        for d in (1, 3, 2):
            total = total + second_in[c][(own_pos + d) % 4]
        value = z_parent[STARTS[c]:STARTS[c] + WIDTHS[c]] - streamed(total, k_high[...], k_low[...])
        x_block[c][cls, t_self] = value
        for d in (2, 1, 3):
            x_copy(c, d).start()
        x_all[STARTS[c]:STARTS[c] + WIDTHS[c]] = value

    def pick_copy(c, f, a):
        return remote(pick_send[c].at[f, a], pick_in[c].at[f, first_pos[f]], t2_s.at[c, f], t2_r.at[c, f], first_dev(f, a))

    def pick_wait(c, f):
        blocks = pick_in[c].at[f, pl.ds(0, 3)]
        return remote(blocks, blocks, t2_s.at[c, f], t2_r.at[c, f], first_dev(f, (first_pos[f] + 1) % 4))

    def step_pick(c):
        x_wait(c).wait_recv()
        for f in range(2):
            for t in range(2):
                picked = chosen(x_block[c][f, t], one_hot[f, t])
                for a in range(4):
                    pick_send[c][f, a, t] = picked[:, a * R:(a + 1) * R]
            pick_in[c][f, first_pos[f]] = pick_send[c][f, first_pos[f]]
            for d in (2, 1, 3):
                pick_copy(c, f, (first_pos[f] + d) % 4).start()

    def v_wait(c, g):
        blocks = v_in[c].at[pl.ds(0, (2, 5)[g])]
        remote(blocks, blocks, v_s.at[c], v_r.at[c, g], (far[0], q)).wait_recv()

    def step_return(c):
        for f in range(2):
            pick_wait(c, f).wait_recv()

        def one(s):
            p = parent_ids[s]
            x_p, y_p = p // 4, p % 4
            f = (x_p + y_p + core) % 2
            a = jnp.where(f == 0, x_p, y_p)
            t = jnp.where(f == 0, y_p, x_p) // 2
            v_send[c][s] = pick_in[c][f, a, t]

        for j in range(7):
            s = partners[j]
            one(s)
            remote(v_send[c].at[s], v_in[c].at[r], v_s.at[c], v_r.at[c, group(j)], (s, q)).start()
        one(r)
        v_in[c][r] = v_send[c][r]

    def send_panels():
        for k in partners[:7]:
            remote(panels.at[k], panel_in.at[r], p_s.at[0], p_r.at[0], (k, q)).start()
        panel_in[r] = panels[r]

    def panel_wait():
        blocks = panel_in.at[pl.ds(0, 7)]
        return remote(blocks, blocks, p_s.at[0], p_r.at[0], (far[0], q))

    def gains():
        panel_wait().wait_recv()

        def one(s):
            high, low = split(product(panel_in[s], inverse[s]))
            gain_high[s] = high
            gain_low[s] = low

        for s in range(CH):
            one(s)

    def solved():
        def one(k):
            value = jnp.concatenate([y_send[c][k] for c in range(C)], axis=0)
            z_child[k] = product(value, inverse[k])

        for k in range(CH):
            one(k)

    def out_copy(h, k):
        return pltpu.make_async_copy(out_buf.at[k, :, pl.ds(h * R, R)], child_out.at[k, :, pl.ds(h * R, R)], out_sem.at[h, k])

    def step_final(c):
        start = STARTS[c]
        end = start + WIDTHS[c]
        half = start // R

        def one(s):
            value = z_child[s, start:end] - streamed(v_in[c][s], gain_high[s], gain_low[s])
            if end % R:
                z_child[s, start:end] = value
            else:
                if start % R:
                    value = jnp.concatenate([z_child[s, half * R:start], value], axis=0)
                out_buf[s, :, half * R:(half + 1) * R] = value.T
                out_copy(half, s).start()

        v_wait(c, 1)
        for s in partners[2:]:
            one(s)
        v_wait(c, 0)
        for s in far:
            one(s)

    x_out = pltpu.make_async_copy(x_all, parent_out, out_sem.at[2, 0])

    def parent_result():
        x_all[...] = x_all[...].T
        x_out.start()

    def v_sent(c):
        blocks = v_in[c].at[pl.ds(0, 7)]
        remote(blocks, blocks, v_s.at[c], v_r.at[c, 0], (far[0], q)).wait_send()

    def sent():
        panel_wait().wait_send()
        for f in range(2):
            rows_wait(f).wait_send()
        for c in range(C):
            blocks = y_in[c].at[pl.ds(0, 7)]
            remote(blocks, blocks, y_s.at[c], y_r.at[c, 0], (far[0], q)).wait_send()
            for f in range(2):
                first_wait(c, f).wait_send()
                pick_wait(c, f).wait_send()
            second_wait(c).wait_send()
            x_wait(c).wait_send()
        for c in range(C - 1):
            v_sent(c)

    steps = dict(U=step_update, D=step_dense, P=step_parent, K=step_pick, R=step_return, F=step_final)
    send_rows()
    for c in range(1, C):
        y_follow(c)
    split_panels()
    send_panels()
    gram()
    make_one_hot()
    for step in ORDER:
        if step == "solved":
            solved()
        elif step == "gains":
            gains()
        elif step == "parent":
            parent_result()
        elif step == "sent":
            sent()
        else:
            steps[step[0]](int(step[1:]))

    v_sent(C - 1)

    for h in range(2):
        for k in range(CH):
            out_copy(h, k).wait()
    x_out.wait()


def hand_over(child, parent, child_out, parent_out, in_sems, out_sems, held, held_parent):
    ins = [pltpu.make_async_copy(child.at[k], held.at[k], in_sems.at[k]) for k in range(CH)]
    ins.append(pltpu.make_async_copy(parent, held_parent, in_sems.at[CH]))
    outs = [pltpu.make_async_copy(held.at[k], child_out.at[k], out_sems.at[k]) for k in range(CH)]
    outs.append(pltpu.make_async_copy(held_parent, parent_out, out_sems.at[CH]))
    for copy in ins:
        copy.start()
    for first, second in zip(ins, outs):
        first.wait()
        second.start()
    for copy in outs:
        copy.wait()


def body(child_inverse, child_rhs, panels, panel_parent, panel_rows, parent_inverse, parent_rhs):
    anywhere = pl.BlockSpec(memory_space=pl.ANY)
    child, parent = pl.pallas_call(
        kernel,
        out_shape=(jax.ShapeDtypeStruct((CH, W, W), F32), jax.ShapeDtypeStruct((W, W), F32)),
        in_specs=[pl.BlockSpec(memory_space=pltpu.SMEM)] + [anywhere] * 6,
        out_specs=(anywhere, anywhere),
        scratch_shapes=list(SCRATCH.values()),
        compiler_params=pltpu.CompilerParams(collective_id=0, has_side_effects=True, vmem_limit_bytes=56 << 20),
        cost_estimate=pl.CostEstimate(flops=2 * 2100 * 10**6, bytes_accessed=8 << 20, transcendentals=0),
    )(
        panel_parent.reshape(CH), child_inverse[0, 0], child_rhs[0, 0], panels[0, 0], panel_rows[0, 0],
        parent_inverse[0, 0], parent_rhs[0, 0],
    )
    child, parent = pl.pallas_call(
        hand_over,
        out_shape=(jax.ShapeDtypeStruct((CH, W, W), F32), jax.ShapeDtypeStruct((W, W), F32)),
        in_specs=[anywhere] * 2,
        out_specs=(anywhere, anywhere),
        scratch_shapes=[DMA((CH + 1,)), DMA((CH + 1,)), pltpu.VMEM((CH, W, W), F32), pltpu.VMEM((W, W), F32)],
    )(child, parent)
    return child[None, None], parent[None, None]


def solution(mesh):
    placed = (
        P("prow", "pcol", None, None, None),
        P("prow", "pcol", None, None, None),
        P("prow", "pcol", None, None, None),
        P("prow", "pcol", None, None),
        P("prow", "pcol", None, None),
        P("prow", "pcol", None, None),
        P("prow", "pcol", None, None),
    )
    return jax.shard_map(
        body,
        mesh=mesh,
        in_specs=placed,
        out_specs=(P("prow", "pcol", None, None, None), P("prow", "pcol", None, None)),
        check_vma=False,
    )
```

```python
import jax
import jax.numpy as jnp
from jax import lax
from jax.experimental import pallas as pl
from jax.experimental.pallas import tpu as pltpu
from jax.sharding import PartitionSpec as P

MESH = pl.DeviceIdType.MESH
F32 = jnp.float32
BF16 = jnp.bfloat16
DMA = pltpu.SemaphoreType.DMA
W = 256
R = 128
CH = 8
WIDTHS = [32, 32, 64, 64, 32, 32]
C = len(WIDTHS)
STARTS = [sum(WIDTHS[:c]) for c in range(C)]

SCRATCH = dict(
    inverse=pltpu.VMEM((CH, W, W), F32),
    rhs=pltpu.VMEM((CH, W, W), F32),
    panels=pltpu.VMEM((CH, R, W), F32),
    rows=pltpu.VMEM((CH, R), jnp.int32),
    pinv=pltpu.VMEM((W, W), F32),
    prhs=pltpu.VMEM((W, W), F32),
    panel_high=pltpu.VMEM((CH, R, W), BF16),
    panel_low=pltpu.VMEM((CH, R, W), BF16),
    rows_send=pltpu.VMEM((2, 4, 8, R), jnp.int32),
    rows_in=pltpu.VMEM((2, 4, 8, R), jnp.int32),
    one_hot=pltpu.VMEM((2, 2, W, 4 * R), BF16),
    k_high=pltpu.VMEM((W, W), BF16),
    k_low=pltpu.VMEM((W, W), BF16),
    z_parent=pltpu.VMEM((W, W), F32),
    x_all=pltpu.VMEM((W, W), F32),
    panel_in=pltpu.VMEM((CH, R, W), F32),
    gain_high=pltpu.VMEM((CH, W, R), BF16),
    gain_low=pltpu.VMEM((CH, W, R), BF16),
    v_in=pltpu.VMEM((CH, W, R), F32),
    z_child=pltpu.VMEM((CH, W, W), F32),
    load_sem=DMA((3, CH)),
    y_s=DMA((C,)), y_r=DMA((C, 2)),
    p_s=DMA((1,)), p_r=DMA((1,)),
    i_s=DMA((2,)), i_r=DMA((2,)),
    s1_s=DMA((C, 2)), s1_r=DMA((C, 2)),
    s2_s=DMA((C,)), s2_r=DMA((C,)),
    t1_s=DMA((C,)), t1_r=DMA((C,)),
    t2_s=DMA((C, 2)), t2_r=DMA((C, 2)),
    v_s=DMA((C,)), v_r=DMA((C, 2)),
)
CHUNKED = dict(
    y_send=(CH, None, W),
    y_in=(CH, None, W),
    update=(CH, None, R),
    first_send=(2, 4, 2, None, R),
    first_in=(2, 4, 2, None, R),
    dense=(2, 2, None, W),
    second_in=(4, None, W),
    x_block=(2, 2, None, W),
    pick_send=(2, 4, 2, None, R),
    pick_in=(2, 4, 2, None, R),
    v_send=(CH, None, R),
)
for name, shape in CHUNKED.items():
    for c in range(C):
        SCRATCH[name + str(c)] = pltpu.VMEM(tuple(WIDTHS[c] if n is None else n for n in shape), F32)
NN = ((1,), (0,))
NT = ((1,), (1,))
TN = ((0,), (0,))

ORDER = [
    "solved", "U0", "U1", "D0", "D1", "P0", "U2", "P1", "K0", "U3",
    "D2", "K1", "R0", "U4", "U5", "D3", "P2", "R1", "D4", "D5",
    "P3", "K2", "P4", "gains", "P5", "parent", "K3", "R2", "K4", "K5",
    "R3", "F2", "R4", "R5", "sent", "F5",
]


def split(value):
    high = value.astype(BF16)
    low = (value - high.astype(F32)).astype(BF16)
    return high, low


def dot(a, b, dims=NN):
    return lax.dot_general(a, b, (dims, ((), ())), preferred_element_type=F32)


def product(a, b, dims=NN):
    a_high, a_low = split(a)
    b_high, b_low = split(b)
    return dot(a_high, b_high, dims) + (dot(a_high, b_low, dims) + dot(a_low, b_high, dims))


def streamed(a, b_high, b_low, dims=NN):
    rows = a.shape[0]
    a_high, a_low = split(a)
    both = dot(jnp.concatenate([a_high, a_low], axis=0), b_high, dims)
    return both[:rows] + (both[rows:] + dot(a_high, b_low, dims))


def chosen(a, one_hot, dims=NN):
    rows = a.shape[0]
    a_high, a_low = split(a)
    both = dot(jnp.concatenate([a_high, a_low], axis=0), one_hot, dims)
    return both[:rows] + both[rows:]


def kernel(parent_ids, inverse_hbm, rhs_hbm, panels_hbm, rows_hbm, pinv_hbm, prhs_hbm, child_out, parent_out, *scratch):
    ref = dict(zip(SCRATCH, scratch))
    inverse = ref["inverse"]
    rhs = ref["rhs"]
    panels = ref["panels"]
    rows = ref["rows"]
    pinv = ref["pinv"]
    prhs = ref["prhs"]
    panel_high = ref["panel_high"]
    panel_low = ref["panel_low"]
    rows_send = ref["rows_send"]
    rows_in = ref["rows_in"]
    one_hot = ref["one_hot"]
    k_high = ref["k_high"]
    k_low = ref["k_low"]
    z_parent = ref["z_parent"]
    x_all = ref["x_all"]
    panel_in = ref["panel_in"]
    gain_high = ref["gain_high"]
    gain_low = ref["gain_low"]
    z_child = ref["z_child"]
    load_sem = ref["load_sem"]
    y_s = ref["y_s"]
    y_r = ref["y_r"]
    p_s = ref["p_s"]
    p_r = ref["p_r"]
    i_s = ref["i_s"]
    i_r = ref["i_r"]
    s1_s = ref["s1_s"]
    s1_r = ref["s1_r"]
    s2_s = ref["s2_s"]
    s2_r = ref["s2_r"]
    t1_s = ref["t1_s"]
    t1_r = ref["t1_r"]
    t2_s = ref["t2_s"]
    t2_r = ref["t2_r"]
    v_s = ref["v_s"]
    v_r = ref["v_r"]
    y_send = [ref["y_send" + str(c)] for c in range(C)]
    y_in = [ref["y_in" + str(c)] for c in range(C)]
    update = [ref["update" + str(c)] for c in range(C)]
    first_send = [ref["first_send" + str(c)] for c in range(C)]
    first_in = [ref["first_in" + str(c)] for c in range(C)]
    dense = [ref["dense" + str(c)] for c in range(C)]
    second_in = [ref["second_in" + str(c)] for c in range(C)]
    x_block = [ref["x_block" + str(c)] for c in range(C)]
    pick_send = [ref["pick_send" + str(c)] for c in range(C)]
    pick_in = [ref["pick_in" + str(c)] for c in range(C)]
    v_send = [ref["v_send" + str(c)] for c in range(C)]
    v_in = ref["v_in"]

    r = lax.axis_index("prow")
    q = lax.axis_index("pcol")
    z, core = r // 2, r % 2
    x, y = q // 4, q % 4
    cls = (x + y + core) % 2
    own_pos = jnp.where(cls == 0, y, x)
    other_pos = jnp.where(cls == 0, x, y)
    t_self = own_pos // 2
    first_pos = (x, y)

    partners = [((z + step) % 4) * 2 + (core + d) % 2 for step, d in ((2, 0), (2, 1), (1, 0), (1, 1), (3, 0), (3, 1), (0, 1), (0, 0))]
    far, near = partners[:2], partners[2:7]

    def first_dev(f, a):
        return (r, a * 4 + y) if f == 0 else (r, x * 4 + a)

    def own_dev(a):
        return (r, jnp.where(cls == 0, x * 4 + a, a * 4 + y))

    def other_dev(a):
        return (r, jnp.where(cls == 0, a * 4 + y, x * 4 + a))

    def remote(src, dst, send, recv, dev):
        return pltpu.make_async_remote_copy(
            src_ref=src, dst_ref=dst, send_sem=send, recv_sem=recv, device_id=dev, device_id_type=MESH
        )

    barrier = pltpu.get_barrier_semaphore()
    for k in partners[:7]:
        pl.semaphore_signal(barrier, inc=1, device_id=(k, q), device_id_type=MESH)
    for f in range(2):
        for d in range(1, 4):
            pl.semaphore_signal(barrier, inc=1, device_id=first_dev(f, (first_pos[f] + d) % 4), device_id_type=MESH)

    def load(k):
        return (
            pltpu.make_async_copy(inverse_hbm.at[k], inverse.at[k], load_sem.at[0, k]),
            pltpu.make_async_copy(rhs_hbm.at[k], rhs.at[k], load_sem.at[1, k]),
        )

    for k in partners:
        for copy in load(k):
            copy.start()
    panel_load = pltpu.make_async_copy(panels_hbm, panels, load_sem.at[2, 0])
    rows_load = pltpu.make_async_copy(rows_hbm, rows, load_sem.at[2, 1])
    pinv_load = pltpu.make_async_copy(pinv_hbm, pinv, load_sem.at[2, 2])
    prhs_load = pltpu.make_async_copy(prhs_hbm, prhs, load_sem.at[2, 3])
    for copy in (rows_load, panel_load, pinv_load, prhs_load):
        copy.start()

    def group(j):
        return 0 if j < 2 else 1

    def y_start(c, j):
        k = partners[j]
        remote(y_send[c].at[k], y_in[c].at[r], y_s.at[c], y_r.at[c, group(j)], (k, q)).start()

    def y_wait(c, g):
        blocks = y_in[c].at[pl.ds(0, (2, 5)[g])]
        remote(blocks, blocks, y_s.at[c], y_r.at[c, g], (far[0], q)).wait_recv()

    def forward(k):
        for copy in load(k):
            copy.wait()
        value = product(inverse[k], rhs[k]).T
        for c in range(C):
            y_send[c][k] = value[STARTS[c]:STARTS[c] + WIDTHS[c]]

    forward(partners[0])
    pl.semaphore_wait(barrier, 13)
    y_start(0, 0)
    for j in range(1, 7):
        forward(partners[j])
        y_start(0, j)
    forward(r)
    for c in range(C):
        y_in[c][r] = y_send[c][r]

    def y_follow(c):
        for j in range(7):
            y_start(c, j)

    def parent_of(f, a, t):
        if f == 0:
            return a * 4 + (a + core) % 2 + 2 * t
        return ((a + core + 1) % 2 + 2 * t) * 4 + a

    def rows_copy(f, a):
        return remote(rows_send.at[f, a], rows_in.at[f, first_pos[f]], i_s.at[f], i_r.at[f], first_dev(f, a))

    def rows_wait(f):
        blocks = rows_in.at[f, pl.ds(0, 3)]
        return remote(blocks, blocks, i_s.at[f], i_r.at[f], first_dev(f, (first_pos[f] + 1) % 4))

    def send_rows():
        rows_load.wait()
        for f in range(2):
            for a in range(4):
                for t in range(2):
                    p = parent_of(f, a, t)
                    listed = jnp.full((1, R), -1, jnp.int32)
                    for s in range(CH):
                        listed = jnp.where(parent_ids[s] == p, rows[s:s + 1, :], listed)
                    rows_send[f, a, t:t + 1, :] = listed
                rows_send[f, a, 2:8, :] = jnp.zeros((6, R), jnp.int32)
            rows_in[f, first_pos[f]] = rows_send[f, first_pos[f]]
            for d in range(1, 4):
                rows_copy(f, (first_pos[f] + d) % 4).start()

    def split_panels():
        panel_load.wait()
        for s in range(CH):
            high, low = split(panels[s])
            panel_high[s] = high
            panel_low[s] = low

    def gram():
        pinv_load.wait()
        prhs_load.wait()
        value = product(pinv[...], pinv[...], TN)
        high, low = split(value)
        k_high[...] = high
        k_low[...] = low
        z_parent[...] = product(value, prhs[...]).T

    def make_one_hot():
        places = lax.broadcasted_iota(jnp.int32, (W, R), 0)
        for f in range(2):
            rows_wait(f).wait_recv()
            for a in range(4):
                for t in range(2):
                    matrix = jnp.where(places == rows_in[f, a, t:t + 1, :], 1.0, 0.0)
                    one_hot[f, t, :, a * R:(a + 1) * R] = matrix.astype(BF16)

    def first_copy(c, f, a):
        return remote(first_send[c].at[f, a], first_in[c].at[f, first_pos[f]], s1_s.at[c, f], s1_r.at[c, f], first_dev(f, a))

    def first_wait(c, f):
        blocks = first_in[c].at[f, pl.ds(0, 3)]
        return remote(blocks, blocks, s1_s.at[c, f], s1_r.at[c, f], first_dev(f, (first_pos[f] + 1) % 4))

    def step_update(c):
        def one(s):
            update[c][s] = streamed(y_in[c][s], panel_high[s], panel_low[s], NT)

        y_wait(c, 1)
        for s in partners[2:]:
            one(s)
        y_wait(c, 0)
        for s in far:
            one(s)
        for f in range(2):
            for a in range(4):
                for t in range(2):
                    p = parent_of(f, a, t)
                    slot = jnp.int32(0)
                    for s in range(1, CH):
                        slot = jnp.where(parent_ids[s] == p, s, slot)
                    first_send[c][f, a, t] = update[c][slot]
            first_in[c][f, first_pos[f]] = first_send[c][f, first_pos[f]]
            for d in (2, 1, 3):
                first_copy(c, f, (first_pos[f] + d) % 4).start()

    def second_own(c):
        a = (own_pos + 2) % 4
        return remote(dense[c].at[cls, 1 - t_self], second_in[c].at[own_pos], s2_s.at[c], s2_r.at[c], own_dev(a))

    def second_other(c, t):
        a = (other_pos + 1) % 2 + 2 * t
        return remote(dense[c].at[1 - cls, t], second_in[c].at[other_pos], s2_s.at[c], s2_r.at[c], other_dev(a))

    def second_wait(c):
        blocks = second_in[c].at[pl.ds(0, 3)]
        return remote(blocks, blocks, s2_s.at[c], s2_r.at[c], own_dev((own_pos + 1) % 4))

    def step_dense(c):
        for f in range(2):
            first_wait(c, f).wait_recv()
            for t in range(2):
                blocks = jnp.concatenate([first_in[c][f, a, t] for a in range(4)], axis=1)
                dense[c][f, t] = chosen(blocks, one_hot[f, t], NT)
        second_own(c).start()
        for t in range(2):
            second_other(c, t).start()

    def x_copy(c, d):
        return remote(x_block[c].at[cls, t_self], x_block[c].at[cls, t_self], t1_s.at[c], t1_r.at[c], own_dev((own_pos + d) % 4))

    def x_wait(c):
        blocks = second_in[c].at[pl.ds(0, 3)]
        return remote(blocks, blocks, t1_s.at[c], t1_r.at[c], own_dev((own_pos + 1) % 4))

    def step_parent(c):
        total = dense[c][cls, t_self]
        second_wait(c).wait_recv()
        for d in (1, 3, 2):
            total = total + second_in[c][(own_pos + d) % 4]
        value = z_parent[STARTS[c]:STARTS[c] + WIDTHS[c]] - streamed(total, k_high[...], k_low[...])
        x_block[c][cls, t_self] = value
        for d in (2, 1, 3):
            x_copy(c, d).start()
        x_all[STARTS[c]:STARTS[c] + WIDTHS[c]] = value

    def pick_copy(c, f, a):
        return remote(pick_send[c].at[f, a], pick_in[c].at[f, first_pos[f]], t2_s.at[c, f], t2_r.at[c, f], first_dev(f, a))

    def pick_wait(c, f):
        blocks = pick_in[c].at[f, pl.ds(0, 3)]
        return remote(blocks, blocks, t2_s.at[c, f], t2_r.at[c, f], first_dev(f, (first_pos[f] + 1) % 4))

    def step_pick(c):
        x_wait(c).wait_recv()
        for f in range(2):
            for t in range(2):
                picked = chosen(x_block[c][f, t], one_hot[f, t])
                for a in range(4):
                    pick_send[c][f, a, t] = picked[:, a * R:(a + 1) * R]
            pick_in[c][f, first_pos[f]] = pick_send[c][f, first_pos[f]]
            for d in (2, 1, 3):
                pick_copy(c, f, (first_pos[f] + d) % 4).start()

    def v_wait(c, g):
        blocks = v_in.at[pl.ds(0, (2, 5)[g]), pl.ds(0, WIDTHS[c])]
        remote(blocks, blocks, v_s.at[c], v_r.at[c, g], (far[0], q)).wait_recv()

    def step_return(c):
        for f in range(2):
            pick_wait(c, f).wait_recv()

        def one(s):
            p = parent_ids[s]
            x_p, y_p = p // 4, p % 4
            f = (x_p + y_p + core) % 2
            a = jnp.where(f == 0, x_p, y_p)
            t = jnp.where(f == 0, y_p, x_p) // 2
            v_send[c][s] = pick_in[c][f, a, t]

        for j in range(7):
            s = partners[j]
            one(s)
            remote(v_send[c].at[s], v_in.at[r, pl.ds(STARTS[c], WIDTHS[c])], v_s.at[c], v_r.at[c, group(j)], (s, q)).start()
        one(r)
        v_in[r, STARTS[c]:STARTS[c] + WIDTHS[c]] = v_send[c][r]

    def send_panels():
        for k in partners[:7]:
            remote(panels.at[k], panel_in.at[r], p_s.at[0], p_r.at[0], (k, q)).start()
        panel_in[r] = panels[r]

    def panel_wait():
        blocks = panel_in.at[pl.ds(0, 7)]
        return remote(blocks, blocks, p_s.at[0], p_r.at[0], (far[0], q))

    def gains():
        panel_wait().wait_recv()

        def one(s):
            high, low = split(product(panel_in[s], inverse[s]).T)
            gain_high[s] = high
            gain_low[s] = low

        for s in range(CH):
            one(s)

    def solved():
        def one(k):
            value = jnp.concatenate([y_send[c][k] for c in range(C)], axis=0)
            z_child[k] = product(value, inverse[k]).T

        for k in range(CH):
            one(k)

    def step_final(c):
        h = STARTS[c] // R
        chunks = [n for n in range(C) if STARTS[n] // R == h]

        def one(s):
            v_high, v_low = split(v_in[s, h * R:(h + 1) * R])
            g_high = gain_high[s]
            term = dot(g_high, v_high, NT) + (dot(g_high, v_low, NT) + dot(gain_low[s], v_high, NT))
            child_out[s, :, h * R:(h + 1) * R] = z_child[s, :, h * R:(h + 1) * R] - term

        for n in chunks:
            v_wait(n, 1)
        for s in partners[2:]:
            one(s)
        for n in chunks:
            v_wait(n, 0)
        for s in far:
            one(s)

    def parent_result():
        parent_out[...] = x_all[...].T

    def v_sent(c):
        blocks = v_in.at[pl.ds(0, 7), pl.ds(0, WIDTHS[c])]
        remote(blocks, blocks, v_s.at[c], v_r.at[c, 0], (far[0], q)).wait_send()

    def sent():
        panel_wait().wait_send()
        for f in range(2):
            rows_wait(f).wait_send()
        for c in range(C):
            blocks = y_in[c].at[pl.ds(0, 7)]
            remote(blocks, blocks, y_s.at[c], y_r.at[c, 0], (far[0], q)).wait_send()
            for f in range(2):
                first_wait(c, f).wait_send()
                pick_wait(c, f).wait_send()
            second_wait(c).wait_send()
            x_wait(c).wait_send()
        for c in range(C - 1):
            v_sent(c)

    steps = dict(U=step_update, D=step_dense, P=step_parent, K=step_pick, R=step_return, F=step_final)
    send_rows()
    for c in range(1, C):
        y_follow(c)
    split_panels()
    send_panels()
    gram()
    make_one_hot()
    for step in ORDER:
        if step == "solved":
            solved()
        elif step == "gains":
            gains()
        elif step == "parent":
            parent_result()
        elif step == "sent":
            sent()
        else:
            steps[step[0]](int(step[1:]))

    v_sent(C - 1)


def body(child_inverse, child_rhs, panels, panel_parent, panel_rows, parent_inverse, parent_rhs):
    anywhere = pl.BlockSpec(memory_space=pl.ANY)
    vmem = pl.BlockSpec(memory_space=pltpu.VMEM)
    child, parent = pl.pallas_call(
        kernel,
        out_shape=(pltpu.VMEM((CH, W, W), F32), pltpu.VMEM((W, W), F32)),
        in_specs=[pl.BlockSpec(memory_space=pltpu.SMEM)] + [anywhere] * 6,
        out_specs=(vmem, vmem),
        scratch_shapes=list(SCRATCH.values()),
        compiler_params=pltpu.CompilerParams(collective_id=0, has_side_effects=True, vmem_limit_bytes=56 << 20),
        cost_estimate=pl.CostEstimate(flops=2 * 2100 * 10**6, bytes_accessed=8 << 20, transcendentals=0),
    )(
        panel_parent.reshape(CH), child_inverse[0, 0], child_rhs[0, 0], panels[0, 0], panel_rows[0, 0],
        parent_inverse[0, 0], parent_rhs[0, 0],
    )
    return child[None, None], parent[None, None]


def solution(mesh):
    placed = (
        P("prow", "pcol", None, None, None),
        P("prow", "pcol", None, None, None),
        P("prow", "pcol", None, None, None),
        P("prow", "pcol", None, None),
        P("prow", "pcol", None, None),
        P("prow", "pcol", None, None),
        P("prow", "pcol", None, None),
    )
    return jax.shard_map(
        body,
        mesh=mesh,
        in_specs=placed,
        out_specs=(P("prow", "pcol", None, None, None), P("prow", "pcol", None, None)),
        check_vma=False,
    )
```
